128 devices in a mesh: depth: 8 (over y_lo, z), rows: 2 (over core), cols: 8 (over x, y_hi).
Axes of the slice: x: 4, y: 4 (y_hi: 2, y_lo: 2; y = y_hi * 2 + y_lo), z: 4, core: 2. Of those that a mesh axis runs over, the one named last changes fastest.
Arguments:
- lower_panels: bfloat16 [16, 8, 768, 1024], P('depth', None, None, ('rows', 'cols')), may hold values from -0.23925781 to 0.23925781
- upper_panels: bfloat16 [16, 1024, 6144], P('depth', 'rows', 'cols'), may hold values from -0.23925781 to 0.23925781
- given_inverse: bfloat16 [16, 1024, 1024], P('depth', 'rows'), may hold values from -0.05625 to 2, as said below
- structure: int32 [16, 48], P('depth'), may hold values 0 or 1
- ancestor_entries: float32 [6144, 6144], P(('depth', 'rows'), 'cols'), may hold values from -0.6 to 19.2, as said below
Outputs:
- column_factor: float32 [6144, 512], P(('depth', 'rows'))
- trailing: float32 [6144, 6144], P(('depth', 'rows'), 'cols')
The draws below stay inside these ranges and needn't reach their ends.
Inputs may be any that keep to these rules, and one draw needn't show every extreme that they name: `given_inverse`: off-diagonal entries are small against the diagonal. `ancestor_entries`: diagonal entries lie between 12.8 and 19.2.
All inputs are finite; a program needn't handle non-finite values. No bound on the sum of `structure` on one device may be relied on, other than what follows from the above.
Results may differ from the reference program's by a relative error of at most 0.0003.
Values may be sent and summed in bfloat16 or wider, within the bound.
A program may use at most 128 MiB of HBM per device.

```python
import jax
import jax.numpy as jnp
from jax import lax

NS = 1024
NA = 6144
PW = 512
BLOCK = 128
NEWTON = 2
NSUB = 16
SPAN = 768
N_DEPTH = 8


def draw_given_inverse(key, part):
    key_diag = jax.random.fold_in(key, 11)
    key_noise = jax.random.fold_in(key, 12)
    diagonal = jnp.exp(jax.random.uniform(key_diag, (NSUB, NS), jnp.float32, jnp.log(0.5), jnp.log(2.0)))
    noise = jnp.clip(jax.random.normal(key_noise, (NSUB, NS, NS), jnp.float32), -6.0, 6.0)
    noise = noise * (0.3 / NS ** 0.5)
    identity = jnp.eye(NS, dtype=jnp.float32)
    return (noise * (1.0 - identity) + identity * diagonal[:, :, None]).astype(jnp.bfloat16)


def draw_ancestor_entries(key, part):
    key_jitter = jax.random.fold_in(key, 21)
    key_noise = jax.random.fold_in(key, 22)
    noise = jnp.clip(jax.random.normal(key_noise, (NA, NA), jnp.float32), -6.0, 6.0) * 0.1
    jitter = jax.random.uniform(key_jitter, (NA,), jnp.float32, -1.0, 1.0)
    identity = jnp.eye(NA, dtype=jnp.float32)
    return noise * (1.0 - identity) + identity * (16.0 * (1.0 + 0.2 * jitter))[:, None]


def set_ends(array, own_key, least, top_value):
    spot = [jax.random.randint(jax.random.fold_in(own_key, axis), (), 0, length) for axis, length in enumerate(array.shape)]
    main_axis = array.shape.index(max(array.shape))
    beside = spot[:main_axis] + [(spot[main_axis] + 1) % array.shape[main_axis]] + spot[main_axis + 1:]
    return array.at[tuple(spot)].set(least).at[tuple(beside)].set(top_value)


def level_of(own_key, shape, split, low, top_value):
    gain = 1.0
    for position, blocks in split:
        draws = jax.random.uniform(jax.random.fold_in(jax.random.fold_in(own_key, 6), position), (blocks,), jnp.float32, low / len(split), top_value / len(split))
        gain = gain * jnp.repeat(jnp.exp(draws), shape[position] // blocks).reshape((-1,) + (1,) * (len(shape) - 1 - position))
    return gain


def gaussian(stream_key, dims, scale, most, pieces=(), kind=jnp.bfloat16):
    level = level_of(stream_key, dims, pieces, -0.22, 0.18) if pieces else 1.0
    result = jax.random.normal(stream_key, dims, jnp.float32) * scale * level
    return jnp.minimum(jnp.maximum(result, -most), most).astype(kind)


def setup_inputs(seed: int = 0) -> dict:
    splits = jax.random.split(jax.random.key(seed), 6)
    return {
        "lower_panels": gaussian(splits[0], (NSUB, N_DEPTH, SPAN, NS), 0.04, 0.23925781, ((0, 8), (3, 16))),
        "upper_panels": gaussian(splits[1], (NSUB, NS, NA), 0.04, 0.23925781, ((0, 8), (1, 2), (2, 8))),
        "given_inverse": draw_given_inverse(jax.random.fold_in(splits[5], 71), 0),
        "structure": set_ends((jax.random.randint(splits[3], (NSUB, NA // BLOCK), 0, 4) < 3).astype(jnp.int32), jax.random.fold_in(splits[3], 1), 0, 1),
        "ancestor_entries": draw_ancestor_entries(jax.random.fold_in(splits[5], 71), 0),
    }


def reference(lower_panels, upper_panels, given_inverse, structure, ancestor_entries):
    highest = lax.Precision.HIGHEST
    kept_rows = jnp.repeat(structure.astype(jnp.float32), BLOCK, axis=1)
    lower_flat = lower_panels.reshape(NSUB, NA, NS)

    def add_subtree(running, members):
        lower_block, upper_block, inverse_block, kept_block = members
        lower_masked = lower_block.astype(jnp.float32) * kept_block[:, None]
        upper_masked = upper_block.astype(jnp.float32) * kept_block[None, :]
        applied = jnp.dot(inverse_block.astype(jnp.float32), upper_masked, precision=highest).astype(jnp.bfloat16)
        return running + jnp.dot(lower_masked, applied.astype(jnp.float32), precision=highest), None

    update, _ = lax.scan(add_subtree, jnp.zeros((NA, NA), jnp.float32), (lower_flat, upper_panels, given_inverse, kept_rows))
    ancestor = ancestor_entries - update
    top_block = ancestor[:PW, :]
    pivot = top_block[:, :PW]
    identity = jnp.eye(PW, dtype=jnp.float32)
    inverse = identity / 16.0
    for sweep in range(NEWTON):
        product = jnp.dot(pivot, inverse, precision=highest)
        inverse = jnp.dot(inverse, 2.0 * identity - product, precision=highest)
    column_factor = jnp.dot(ancestor[:, :PW], inverse, precision=highest)
    trailing = ancestor - jnp.dot(column_factor, top_block, precision=highest)
    return column_factor, trailing
```

```python
import functools

import jax
import jax.numpy as jnp
from jax import lax
from jax.experimental import pallas as pl
from jax.experimental.pallas import tpu as pltpu
from jax.sharding import PartitionSpec as P

PW = 512
BLOCK = 128
MESH = pl.DeviceIdType.MESH
VMEM = pl.BlockSpec(memory_space=pltpu.VMEM)
LIMIT = 56 * 1024 * 1024
OFFSETS = (2, 1, 3, 0)
TOP = 32000.0


def place():
    depth, rows, cols = lax.axis_index("depth"), lax.axis_index("rows"), lax.axis_index("cols")
    return depth // 4, depth % 4, rows, cols // 2, cols % 2


def device(low, z, core, x, half):
    return (low * 4 + z, core, x * 2 + half)


def quantize(value):
    most = jnp.maximum(jnp.max(jnp.abs(value), axis=0, keepdims=True), 1e-30)
    return jnp.round(value * (TOP / most)).astype(jnp.int16), most / TOP


def update_kernel(
    low_ref, up_ref, inv_ref, mask_ref, ent_ref, out_ref,
    up_other, app, lg, cq, cs, rq, rs, own, sq, ss, tq, ts,
    up_sem, l1_sem, loc_sem, l2_sem, f_sem, core_sem, half_sem, fwd_sem,
    r1_sem, r1s_sem, r2_sem, r2s_sem,
):
    low, z, core, x, half = place()

    def remote(src, dst, sems, index, target):
        return pltpu.make_async_remote_copy(
            src_ref=src, dst_ref=dst, send_sem=sems.at[0, index], recv_sem=sems.at[1, index],
            device_id=target, device_id_type=MESH,
        )

    partner = device(low, z, 1 - core, x, half)
    across = device(low, z, core, x, 1 - half)
    across_core = device(low, z, 1 - core, x, 1 - half)
    right = device(low, z, core, (x + 1) % 4, half)
    left = device(low, z, core, (x + 3) % 4, half)
    along_z = {o: device(low, (z + o) % 4, core, x, half) for o in (1, 2, 3)}
    along_y = [
        across,
        device(1 - low, z, core, x, half),
        device(1 - low, z, core, x, 1 - half),
    ]

    barrier = pltpu.get_barrier_semaphore()
    friends = [partner, across, across_core, right, left, *along_z.values(), *along_y[1:]]
    for friend in friends:
        pl.semaphore_signal(barrier, inc=1, device_id=friend, device_id_type=MESH)
    pl.semaphore_wait(barrier, len(friends))

    upper_copy = remote(up_ref, up_other, up_sem, 0, partner)
    upper_copy.start()

    lane = pl.multiple_of((x * 4 + core * 2 + half) * 128, 128)
    stage1, kept = [], []
    for q, o in enumerate(OFFSETS):
        owner = (z + o) % 4
        here = pltpu.make_async_copy(
            low_ref.at[owner, core, half], lg.at[q, :, pl.ds(lane, 128)], loc_sem.at[q]
        )
        here.start()
        kept.append(here)
        sends = []
        for t, (target, r, h) in enumerate((
            (across, core, 1 - half), (across_core, 1 - core, 1 - half), (partner, 1 - core, half),
        )):
            copy = remote(
                low_ref.at[owner, r, h], lg.at[q, :, pl.ds(lane, 128)], l1_sem, q * 3 + t, target
            )
            copy.start()
            sends.append(copy)
        stage1.append(sends)

    upper_copy.wait()
    mine, theirs = pl.multiple_of(core * 512, 512), pl.multiple_of((1 - core) * 512, 512)
    for s in range(2):

        @pl.loop(0, 3)
        def _(tile):
            cols = pl.ds(pl.multiple_of(tile * 256, 256), 256)
            total = jnp.dot(
                inv_ref[s, :, pl.ds(mine, 512)], up_ref[s, :, cols], preferred_element_type=jnp.float32
            ) + jnp.dot(
                inv_ref[s, :, pl.ds(theirs, 512)], up_other[s, :, cols], preferred_element_type=jnp.float32
            )
            applied = (total * mask_ref[s:s + 1, cols]).astype(jnp.bfloat16)
            for c in range(8):
                app[half, c // 2, core, (c % 2) * 128 + s * 64:(c % 2) * 128 + s * 64 + 64, cols] = (
                    applied[c * 64:(c + 1) * 64]
                )

    core_copy = remote(app.at[half, :, core], app.at[half, :, core], core_sem, 0, partner)
    core_copy.start()
    half_copies = []
    for p in range(2):
        part = app.at[half, pl.ds(p * 2, 2), core]
        copy = remote(part, part, half_sem, p, across)
        copy.start()
        half_copies.append(copy)

    def ring(q):
        kept[q].wait()
        for copy in stage1[q]:
            copy.wait_recv()
        block = lg.at[q, :, pl.ds(pl.multiple_of(x * 512, 512), 512)]
        copies = [remote(block, block, l2_sem, q * 2, right), remote(block, block, l2_sem, q * 2 + 1, left)]
        for copy in copies:
            copy.start()
        return copies

    def forward(q):
        from_left = pl.multiple_of(((x + 3) % 4) * 512, 512)
        from_right = pl.multiple_of(((x + 1) % 4) * 512, 512)
        first = lg.at[q, pl.ds(0, 192), pl.ds(from_left, 512)]
        second = lg.at[q, pl.ds(192, 192), pl.ds(from_right, 512)]
        copies = [remote(first, first, f_sem, q * 2, right), remote(second, second, f_sem, q * 2 + 1, left)]
        for copy in copies:
            copy.start()
        return copies

    def contribute(q, side):
        o = OFFSETS[q]

        @pl.loop(0, 3)
        def _(tile):
            cols = pl.ds(pl.multiple_of(tile * 256, 256), 256)
            total = jnp.dot(
                lg[q], app[side, :, :, :, cols].reshape(2048, 256), preferred_element_type=jnp.float32
            )
            if o == 0:
                own[side, :, cols] = total
            else:
                values, scale = quantize(total)
                cq[o - 1, side, :, cols] = values
                cs[o - 1, side, :, cols] = jnp.broadcast_to(scale, (8, 256))

        if o == 0:
            return []
        turn = (o - 1) * 2
        return [
            (cq.at[o - 1, side], rq.at[o - 1, side], r1_sem, turn, along_z[o]),
            (cs.at[o - 1, side], rs.at[o - 1, side], r1s_sem, turn, along_z[o]),
        ]

    sent = []

    def give(q, own_side):
        side = half if own_side else 1 - half
        for src, dst, sems, turn, target in contribute(q, side):
            copy = remote(src, dst, sems, turn + (0 if own_side else 1), target)
            copy.start()
            sent.append(copy)

    stage2, passed = {}, {}
    stage2[0] = ring(0)
    core_copy.wait_recv()
    for q in range(4):
        for copy in stage2[q]:
            copy.wait_recv()
        passed[q] = forward(q)
        if q < 3:
            stage2[q + 1] = ring(q + 1)
        if q > 0:
            for copy in passed[q - 1]:
                copy.wait_recv()
            give(q - 1, True)
    forwards = []
    for p, copy in enumerate(half_copies):
        copy.wait_recv()
        part = app.at[1 - half, pl.ds(p * 2, 2), core]
        onward = remote(part, part, fwd_sem, p, partner)
        onward.start()
        forwards.append(onward)
    for copy in forwards:
        copy.wait_recv()
    for q in range(3):
        give(q, False)
    for copy in passed[3]:
        copy.wait_recv()
    give(3, True)
    give(3, False)

    for copy in sent:
        copy.wait_recv()
    moved = []
    here = None
    for t, (row, col) in enumerate((
        (low, 1 - half), (1 - low, half), (1 - low, 1 - half), (low, half),
    )):
        rows = pl.ds(pl.multiple_of(row * 192, 192), 192)
        total = own[col, rows, :]
        for o in range(3):
            total = total + rq[o, col, rows, :].astype(jnp.float32) * rs[o, col, 0:1, :]
        if t < 3:
            values, scale = quantize(total)
            sq[t] = values
            ss[t] = jnp.broadcast_to(scale, (8, 768))
            for copy in (
                remote(sq.at[t], tq.at[t], r2_sem, t, along_y[t]),
                remote(ss.at[t], ts.at[t], r2s_sem, t, along_y[t]),
            ):
                copy.start()
                moved.append(copy)
        else:
            own[col, rows, :] = total
    for copy in moved:
        copy.wait_recv()

    def arrived(t):
        return tq[t].astype(jnp.float32) * ts[t, 0:1, :]

    mine = pl.ds(pl.multiple_of(half * 192, 192), 192)
    other = pl.ds(pl.multiple_of((1 - half) * 192, 192), 192)
    kept_rows = pl.ds(pl.multiple_of(low * 192, 192), 192)
    out_ref[mine, :] = ent_ref[mine, :] - (own[half, kept_rows, :] + arrived(1))
    out_ref[other, :] = ent_ref[other, :] - (arrived(0) + arrived(2))

    upper_sends = [c for sends in stage1 for c in sends]
    for group in (upper_sends, *stage2.values(), *passed.values(), [core_copy], half_copies, forwards, sent, moved):
        for copy in group:
            copy.wait_send()


def split(value):
    high = value.astype(jnp.bfloat16)
    return high, (value - high.astype(jnp.float32)).astype(jnp.bfloat16)


def dot3(a, b):
    (ah, al), (bh, bl) = split(a), split(b)
    dot = functools.partial(jnp.dot, preferred_element_type=jnp.float32)
    return dot(ah, bh) + (dot(ah, bl) + dot(al, bh))


def panel_kernel(
    anc_ref, cf_ref, out_ref, top, cf, top_sem, tg_sem, core_sem, cf_sem, cg_sem, loc_sem
):
    depth, core, col = lax.axis_index("depth"), lax.axis_index("rows"), lax.axis_index("cols")

    def remote(src, dst, sems, index, target):
        return pltpu.make_async_remote_copy(
            src_ref=src, dst_ref=dst, send_sem=sems.at[0, index], recv_sem=sems.at[1, index],
            device_id=target, device_id_type=MESH,
        )

    barrier = pltpu.get_barrier_semaphore()
    friends = [((depth + o // 2) % 8, core if o % 2 == 0 else 1 - core, col) for o in range(1, 16)]
    friends += [(depth, core, (col + o) % 8) for o in range(1, 8)]
    for friend in friends:
        pl.semaphore_signal(barrier, inc=1, device_id=friend, device_id_type=MESH)
    pl.semaphore_wait(barrier, len(friends))

    def piece_copy(p):
        row = p * 32 - (0 if p < 12 else 384)
        return remote(
            anc_ref.at[pl.ds(row, 32)], top.at[p // 2, p % 2], top_sem, p, (p // 2, p % 2, col)
        )

    first_piece = pltpu.make_async_copy(anc_ref.at[pl.ds(0, 32)], top.at[0, 0], loc_sem)

    @pl.when((depth == 0) & (core == 0))
    def _():
        for p in range(1, 12):
            piece_copy(p).start()
        first_piece.start()
        first_piece.wait()

    @pl.when((depth == 0) & (core == 1))
    def _():
        for p in range(12, 16):
            piece_copy(p).start()

    for p in range(1, 16):

        @pl.when((depth == p // 2) & (core == p % 2))
        def _():
            piece_copy(p).wait_recv()

    gathers = []
    for o in range(1, 8):
        piece = top.at[depth, core]
        copy = remote(piece, piece, tg_sem, o - 1, ((depth + o) % 8, core, col))
        copy.start()
        gathers.append(copy)
    for copy in gathers:
        copy.wait_recv()
    side = top.at[:, core]
    core_copy = remote(side, side, core_sem, 0, (depth, 1 - core, col))
    core_copy.start()
    core_copy.wait_recv()

    def cf_copy(o):
        piece = cf.at[o]
        return remote(piece, piece, cf_sem, o, (depth, core, o))

    def zero_copy(o):
        piece = cf.at[0]
        return remote(piece, piece, cf_sem, 7 + o, (depth, core, o))

    @pl.when(col == 0)
    def _():
        row = lax.broadcasted_iota(jnp.int32, (PW, PW), 0)
        identity = (row == lax.broadcasted_iota(jnp.int32, (PW, PW), 1)).astype(jnp.float32)
        pivot = top[:, :, :, :PW].reshape(PW, PW)
        error = identity - pivot * (1.0 / 16.0)
        square = dot3(error, error)
        inverse = dot3(identity + error, identity + square) * (1.0 / 16.0)
        cf[...] = dot3(anc_ref[:, :PW], inverse).reshape(8, 48, PW)
        for o in range(1, 8):
            cf_copy(o).start()
            zero_copy(o).start()
        for o in range(1, 8):
            cf_copy(o).wait_send()
            zero_copy(o).wait_send()

    def ring_copy(o, target):
        piece = cf.at[col]
        return remote(piece, piece, cg_sem, o - 1, (depth, core, target))

    for c in range(1, 8):

        @pl.when(col == c)
        def _():
            cf_copy(c).wait_recv()
            copies = []
            for o in range(1, 7):
                copy = ring_copy(o, (c - 1 + o) % 7 + 1)
                copy.start()
                copies.append(copy)
            zero_copy(c).wait_recv()
            for copy in copies:
                copy.wait()

    factor = cf[...].reshape(384, PW)
    cf_ref[...] = factor
    fh, fl = split(factor)
    dot = functools.partial(jnp.dot, preferred_element_type=jnp.float32)
    for tile in range(3):
        cols = slice(tile * 256, tile * 256 + 256)
        th, tl = split(top[:, :, :, cols].reshape(PW, 256))
        out_ref[:, cols] = anc_ref[:, cols] - (dot(fh, th) + (dot(fh, tl) + dot(fl, th)))

    for copy in (*gathers, core_copy):
        copy.wait_send()

    @pl.when((depth == 0) & (core == 0))
    def _():
        for p in range(1, 12):
            piece_copy(p).wait_send()

    @pl.when((depth == 0) & (core == 1))
    def _():
        for p in range(12, 16):
            piece_copy(p).wait_send()


def sems(count):
    return pltpu.SemaphoreType.DMA((2, count))


def local(lower_panels, upper_panels, given_inverse, structure, ancestor_entries):
    kept = (structure != 0).astype(jnp.bfloat16)
    kept_rows = jnp.repeat(kept, BLOCK, axis=1)
    lower = lower_panels * kept_rows.reshape(2, 8, 768)[..., None]
    lower = lower.reshape(2, 2, 4, 2, 2, 192, 64).transpose(2, 3, 4, 1, 5, 0, 6).reshape(4, 2, 2, 384, 128)
    col_mask = lax.dynamic_slice_in_dim(kept_rows, lax.axis_index("cols") * 768, 768, 1).astype(jnp.float32)
    f32, bf16, i16 = jnp.float32, jnp.bfloat16, jnp.int16
    ancestor = pl.pallas_call(
        update_kernel,
        name="update",
        out_shape=jax.ShapeDtypeStruct((384, 768), f32),
        in_specs=[VMEM] * 5,
        out_specs=VMEM,
        scratch_shapes=[
            pltpu.VMEM((2, 512, 768), bf16),
            pltpu.VMEM((2, 4, 2, 256, 768), bf16),
            pltpu.VMEM((4, 384, 2048), bf16),
            pltpu.VMEM((3, 2, 384, 768), i16),
            pltpu.VMEM((3, 2, 8, 768), f32),
            pltpu.VMEM((3, 2, 384, 768), i16),
            pltpu.VMEM((3, 2, 8, 768), f32),
            pltpu.VMEM((2, 384, 768), f32),
            pltpu.VMEM((3, 192, 768), i16),
            pltpu.VMEM((3, 8, 768), f32),
            pltpu.VMEM((3, 192, 768), i16),
            pltpu.VMEM((3, 8, 768), f32),
            sems(1), sems(12), pltpu.SemaphoreType.DMA((4,)), sems(8), sems(8), sems(1), sems(2), sems(2),
            sems(6), sems(6), sems(3), sems(3),
        ],
        compiler_params=pltpu.CompilerParams(collective_id=0, has_side_effects=True, vmem_limit_bytes=LIMIT),
    )(lower, upper_panels, given_inverse, col_mask, ancestor_entries)
    return pl.pallas_call(
        panel_kernel,
        name="panel",
        out_shape=(jax.ShapeDtypeStruct((384, PW), f32), jax.ShapeDtypeStruct((384, 768), f32)),
        in_specs=[VMEM],
        out_specs=(VMEM, VMEM),
        scratch_shapes=[
            pltpu.VMEM((8, 2, 32, 768), f32),
            pltpu.VMEM((8, 48, PW), f32),
            sems(16), sems(7), sems(1), sems(15), sems(7), pltpu.SemaphoreType.DMA,
        ],
        compiler_params=pltpu.CompilerParams(collective_id=1, has_side_effects=True, vmem_limit_bytes=LIMIT),
    )(ancestor)


def solution(mesh):
    return jax.shard_map(
        local,
        mesh=mesh,
        in_specs=(
            P("depth", None, None, ("rows", "cols")),
            P("depth", "rows", "cols"),
            P("depth", "rows", None),
            P("depth", None),
            P(("depth", "rows"), "cols"),
        ),
        out_specs=(P(("depth", "rows"), None), P(("depth", "rows"), "cols")),
        check_vma=False,
    )
```

```python
import functools

import jax
import jax.numpy as jnp
from jax import lax
from jax.experimental import pallas as pl
from jax.experimental.pallas import tpu as pltpu
from jax.sharding import PartitionSpec as P

PW = 512
MESH = pl.DeviceIdType.MESH
VMEM = pl.BlockSpec(memory_space=pltpu.VMEM)
LIMIT = 58 * 1024 * 1024
OFFSETS = (2, 1, 3, 0)
TOP = 32000.0


def place():
    depth, rows, cols = lax.axis_index("depth"), lax.axis_index("rows"), lax.axis_index("cols")
    return depth // 4, depth % 4, rows, cols // 2, cols % 2


def device(low, z, core, x, half):
    return (low * 4 + z, core, x * 2 + half)


def quantize(value, axis):
    most = jnp.maximum(jnp.max(jnp.abs(value), axis=axis, keepdims=True), 1e-30)
    return jnp.round(value * (TOP / most)).astype(jnp.int16), most / TOP


def split(value):
    high = value.astype(jnp.bfloat16)
    return high, (value - high.astype(jnp.float32)).astype(jnp.bfloat16)


def product(a, b):
    return jnp.dot(a, b, preferred_element_type=jnp.float32)


def dot3(a, b):
    (ah, al), (bh, bl) = split(a), split(b)
    return product(ah, bh) + (product(ah, bl) + product(al, bh))


def received(copies):
    for copy in copies:
        copy.wait_recv()


def whole_kernel(
    kept_ref, low_ref, up_ref, inv_ref, ent_ref, cf_ref, out_ref,
    up_other, turned, turned_top, app, lg, lg_top, cq, cs, rq, rs, own, sq, ss, tq, ts,
    ent_top, ctop, rtop, stop, ttop, top, top_high, top_low, inverse, cf,
    up_sem, l1_sem, loc_sem, l2_sem, f_sem, core_sem, half_sem, fwd_sem,
    r1_sem, r1s_sem, r1b_sem, r1bs_sem, r2_sem, r2s_sem,
    ent_sem, rt_sem, r2t_sem, tg_sem, tc_sem, cf_sem, cg_sem,
):
    low, z, core, x, half = place()
    depth, col = low * 4 + z, x * 2 + half

    def remote(src, dst, sems, index, target):
        return pltpu.make_async_remote_copy(
            src_ref=src, dst_ref=dst, send_sem=sems.at[0, index], recv_sem=sems.at[1, index],
            device_id=target, device_id_type=MESH,
        )

    partner = device(low, z, 1 - core, x, half)
    across = device(low, z, core, x, 1 - half)
    across_core = device(low, z, 1 - core, x, 1 - half)
    right = device(low, z, core, (x + 1) % 4, half)
    left = device(low, z, core, (x + 3) % 4, half)
    along_z = {o: device(low, (z + o) % 4, core, x, half) for o in (1, 2, 3)}
    along_y = [
        across,
        device(1 - low, z, core, x, half),
        device(1 - low, z, core, x, 1 - half),
    ]

    barrier = pltpu.get_barrier_semaphore()
    friends = [((depth + o // 2) % 8, core if o % 2 == 0 else 1 - core, col) for o in range(1, 16)]
    friends += [(depth, core, (col + o) % 8) for o in range(1, 8)]
    friends += [across_core, along_y[2]]
    for friend in friends:
        pl.semaphore_signal(barrier, inc=1, device_id=friend, device_id_type=MESH)
    pl.semaphore_wait(barrier, len(friends))

    upper_copy = remote(up_ref, up_other, up_sem, 0, partner)
    upper_copy.start()

    def entry_copy(g, row):
        target = ((g % 2) * 4 + (g // 2) % 4, g // 16, col)
        return pltpu.make_async_remote_copy(
            src_ref=ent_ref.at[pl.ds(pl.multiple_of(row * 16, 16), 16)], dst_ref=ent_top.at[(g // 8) % 2],
            send_sem=ent_sem.at[0, g], recv_sem=ent_sem.at[1, (g // 8) % 2],
            device_id=target, device_id_type=MESH,
        )

    holder = [(depth == 0) & (core == c) for c in range(2)]
    groups = ([g for g in range(24) if g not in (0, 8)], [g for g in range(25, 32)])
    stays = ([(0, 0), (8, 1)], [(24, 1)])

    def entries(act):
        for c in range(2):

            @pl.when(holder[c])
            def _():
                for g in groups[c]:
                    act(entry_copy(g, g - 24 * c))

    entries(lambda copy: copy.start())
    for c in range(2):

        @pl.when(holder[c])
        def _():
            for g, h in stays[c]:
                row = (g - 24 * c) * 16
                ent_top[h] = ent_ref[row:row + 16, :]

    def factor(s, block):
        return jnp.full((1, 128), kept_ref[s, block].astype(jnp.float32), jnp.float32)

    lane = pl.multiple_of((x * 4 + core * 2 + half) * 128, 128)
    sharers = ((across, core, 1 - half), (across_core, 1 - core, 1 - half), (partner, 1 - core, half))

    def turn_over(j, part):
        lanes = slice(part * 128, part * 128 + 128)
        both = jnp.concatenate(
            [low_ref[s, j, :, lanes] * factor(s, j * 6 + part).astype(jnp.bfloat16) for s in range(2)]
        )
        return both.T

    def share(src, dst, first):
        here = pltpu.make_async_copy(src(core, half), dst, loc_sem.at[first // 3])
        here.start()
        sends = []
        for t, (target, r, h) in enumerate(sharers):
            copy = remote(src(r, h), dst, l1_sem, first + t, target)
            copy.start()
            sends.append(copy)
        return here, sends

    def exchange_top():
        for part in range(4):
            turned_top[part // 2, part % 2] = turn_over(0, part)
        return share(lambda r, h: turned_top.at[r, h], lg_top.at[:, pl.ds(lane, 128)], 24)

    def exchange(q):
        j = (q % 2) * 4 + (z + OFFSETS[q // 2]) % 4
        for part in range(6):
            value = turn_over(j, part)
            for piece in range(2):
                row = part * 128 + piece * 64
                turned[q, row // 384, (row // 192) % 2, row % 192:row % 192 + 64] = (
                    value[piece * 64:piece * 64 + 64]
                )
        return share(lambda r, h: turned.at[q, r, h], lg.at[q, :, pl.ds(lane, 128)], q * 3)

    mine, theirs = pl.multiple_of(core * 512, 512), pl.multiple_of((1 - core) * 512, 512)

    def apply(tile):
        cols = slice(tile * 256, tile * 256 + 256)
        for s in range(2):
            total = product(inv_ref[s, :, pl.ds(mine, 512)], up_ref[s, :, cols]) + product(
                inv_ref[s, :, pl.ds(theirs, 512)], up_other[s, :, cols]
            )
            block = col * 6 + tile * 2
            mask = jnp.concatenate([factor(s, block), factor(s, block + 1)], axis=1)
            applied = (total * mask).astype(jnp.bfloat16)
            for c in range(8):
                app[half, tile, c // 2, core, (c % 2) * 128 + s * 64:(c % 2) * 128 + s * 64 + 64] = (
                    applied[c * 64:(c + 1) * 64]
                )
        part = app.at[half, tile, :, core]
        copies = [remote(part, part, core_sem, tile, partner), remote(part, part, half_sem, tile, across)]
        for copy in copies:
            copy.start()
        return copies

    def forward_applied(tile):
        part = app.at[1 - half, tile, :, core]
        copy = remote(part, part, fwd_sem, tile, partner)
        copy.start()
        return copy

    at_home = pl.ds(pl.multiple_of(x * 512, 512), 512)
    from_left = pl.ds(pl.multiple_of(((x + 3) % 4) * 512, 512), 512)
    from_right = pl.ds(pl.multiple_of(((x + 1) % 4) * 512, 512), 512)

    def both_ways(first, second, sems, q):
        copies = [remote(first, first, sems, q * 2, right), remote(second, second, sems, q * 2 + 1, left)]
        for copy in copies:
            copy.start()
        return copies

    def rows_of(q):
        return (lg_top, 64) if q == 8 else (lg.at[q], 96)

    def ring(q):
        block = rows_of(q)[0].at[:, at_home]
        return both_ways(block, block, l2_sem, q)

    def forward(q):
        rows, count = rows_of(q)
        return both_ways(
            rows.at[pl.ds(0, count), from_left], rows.at[pl.ds(count, count), from_right], f_sem, q
        )

    sides = (half, 1 - half)

    def own_copies(q):
        o, b = OFFSETS[q // 2], q % 2
        return (
            remote(cq.at[o - 1, b, 0], rq.at[o - 1, b, 0], r1_sem, q, along_z[o]),
            remote(cs.at[o - 1, b, 0], rs.at[o - 1, b, 0], r1s_sem, q, along_z[o]),
        )

    def give_own(q):
        o, b = OFFSETS[q // 2], q % 2

        @pl.loop(0, 3)
        def _(tile):
            total = product(lg[q], app[half, tile].reshape(2048, 256))
            if o == 0:
                own[0, tile, b] = total
            else:
                values, scale = quantize(total, 0)
                cq[o - 1, b, 0, tile] = values
                cs[o - 1, b, 0, tile] = jnp.broadcast_to(scale, (8, 256))

        if o != 0:
            for copy in own_copies(q):
                copy.start()

    def other_copies(g, tile):
        o = OFFSETS[g]
        return (
            remote(cq.at[o - 1, :, 1, tile], rq.at[o - 1, :, 1, tile], r1b_sem, g * 3 + tile, along_z[o]),
            remote(cs.at[o - 1, :, 1, tile], rs.at[o - 1, :, 1, tile], r1bs_sem, g * 3 + tile, along_z[o]),
        )

    def give_other(g, tile):
        o = OFFSETS[g]
        total = product(
            lg[g * 2:g * 2 + 2].reshape(384, 2048), app[1 - half, tile].reshape(2048, 256)
        ).reshape(2, 192, 256)
        if o == 0:
            own[1, tile] = total
            return
        values, scale = quantize(total, 1)
        for b in range(2):
            cq[o - 1, b, 1, tile] = values[b]
            cs[o - 1, b, 1, tile] = jnp.broadcast_to(scale[b], (8, 256))
        for copy in other_copies(g, tile):
            copy.start()

    def make_top(turn, tile):
        total = product(lg_top[...], app[sides[turn], tile].reshape(2048, 256))
        ctop[turn, :, :, :, tile * 256:tile * 256 + 256] = total.reshape(4, 2, 16, 256)

    def top_copies(turn):
        return [
            remote(ctop.at[turn, (z + o) % 4], rtop.at[o - 1, turn], rt_sem, turn * 3 + o - 1, along_z[o])
            for o in (1, 2, 3)
        ]

    def give_top(turn):
        copies = top_copies(turn)
        for copy in copies:
            copy.start()
        return copies

    stage1, stage2, passed, applied, onward, tops = {}, {}, {}, {}, {}, {}

    def start_ring(q):
        stage1[q][0].wait()
        received(stage1[q][1])
        stage2[q] = ring(q)

    stage1[8] = exchange_top()
    stage1[0] = exchange(0)
    upper_copy.wait()
    applied[0] = apply(0)
    start_ring(8)
    start_ring(0)
    stage1[1] = exchange(1)
    applied[1] = apply(1)
    start_ring(1)
    stage1[2] = exchange(2)
    applied[2] = apply(2)
    received(stage2[8])
    passed[8] = forward(8)

    for q in range(8):
        received(stage2[q])
        passed[q] = forward(q)
        if q + 2 < 8:
            start_ring(q + 2)
        if q + 3 < 8:
            stage1[q + 3] = exchange(q + 3)
        if q == 0:
            received([applied[t][0] for t in range(3)])
            received(passed[8])
            for tile in range(3):
                make_top(0, tile)
            tops[0] = give_top(0)
        else:
            received(passed[q - 1])
            give_own(q - 1)
        if q == 3:
            applied[0][1].wait_recv()
            onward[0] = forward_applied(0)
        if q == 4:
            onward[0].wait_recv()
            make_top(1, 0)
            give_other(0, 0)
        if q == 5:
            applied[1][1].wait_recv()
            onward[1] = forward_applied(1)
            give_other(1, 0)
        if q == 6:
            onward[1].wait_recv()
            make_top(1, 1)
            give_other(0, 1)
            give_other(1, 1)
            give_other(2, 0)
        if q == 7:
            applied[2][1].wait_recv()
            onward[2] = forward_applied(2)
            give_other(2, 1)
    onward[2].wait_recv()
    make_top(1, 2)
    tops[1] = give_top(1)
    for g in range(3):
        give_other(g, 2)
    received(passed[7])
    give_own(7)

    received(tops[0])
    received(tops[1])
    for turn in range(2):
        total = ctop[turn, z]
        for o in range(3):
            total = total + rtop[o, turn]
        stop[turn] = total
    top_moves = [
        remote(stop.at[turn, row], ttop.at[t], r2t_sem, t, along_y[t])
        for t, (turn, row) in enumerate(((1, low), (0, 1 - low), (1, 1 - low)))
    ]
    for copy in top_moves:
        copy.start()
    for tile in range(3):
        give_other(3, tile)

    def chunk_sum(turn, row, tile):
        total = own[turn, tile, row]
        for o in range(3):
            total = total + rq[o, row, turn, tile].astype(jnp.float32) * rs[o, row, turn, tile, 0:1, :]
        return total

    moved = []

    def hand(t, turn, row, tile):
        values, scale = quantize(chunk_sum(turn, row, tile), 0)
        sq[t, tile] = values
        ss[t, tile] = jnp.broadcast_to(scale, (8, 256))
        copies = [
            remote(sq.at[t, tile], tq.at[t, tile], r2_sem, t * 3 + tile, along_y[t]),
            remote(ss.at[t, tile], ts.at[t, tile], r2s_sem, t * 3 + tile, along_y[t]),
        ]
        for copy in copies:
            copy.start()
        moved.extend(copies)

    for q in range(6):
        received(own_copies(q))
    for tile in range(3):
        hand(1, 0, 1 - low, tile)

    received(top_moves)
    @pl.when((depth != 0) | (core != 0))
    def _():
        for h in range(2):

            @pl.when((depth != 0) | (h == 0))
            def _():
                pltpu.make_async_remote_copy(
                    src_ref=ent_ref.at[pl.ds(0, 16)], dst_ref=ent_top.at[h],
                    send_sem=ent_sem.at[0, 0], recv_sem=ent_sem.at[1, h],
                    device_id=partner, device_id_type=MESH,
                ).wait_recv()

    top[core, half, z, low] = ent_top[half] - (stop[0, low] + ttop[1])
    top[core, 1 - half, z, low] = ent_top[1 - half] - (ttop[0] + ttop[2])
    gathers = []
    for o in range(1, 8):
        piece = top.at[core, :, z, low]
        copy = remote(piece, piece, tg_sem, o - 1, ((depth + o) % 8, core, col))
        copy.start()
        gathers.append(copy)

    for tile in range(3):
        for g in range(3):
            received(other_copies(g, tile))
        hand(0, 1, low, tile)
        hand(2, 1, 1 - low, tile)
        if tile == 0:
            received(gathers)
            core_copy = remote(top.at[core], top.at[core], tc_sem, 0, partner)
            core_copy.start()
    core_copy.wait_recv()

    @pl.when(col == 0)
    def _():
        row = lax.broadcasted_iota(jnp.int32, (PW, PW), 0)
        identity = (row == lax.broadcasted_iota(jnp.int32, (PW, PW), 1)).astype(jnp.float32)
        pivot = top[:, :, :, :, :, :PW].reshape(PW, PW)
        error = identity - pivot * (1.0 / 16.0)
        square = dot3(error, error)
        inverse[...] = dot3(identity + error, identity + square) * (1.0 / 16.0)

    def arrived(t, tile):
        return tq[t, tile].astype(jnp.float32) * ts[t, tile, 0:1, :]

    mine = pl.ds(pl.multiple_of(half * 192, 192), 192)
    other = pl.ds(pl.multiple_of((1 - half) * 192, 192), 192)
    received(moved[0:6])
    for tile in range(3):
        cols = slice(tile * 256, tile * 256 + 256)
        out_ref[mine, cols] = ent_ref[mine, cols] - (chunk_sum(0, low, tile) + arrived(1, tile))
    for tile in range(3):
        received(moved[6 + tile * 4:10 + tile * 4])
        cols = slice(tile * 256, tile * 256 + 256)
        out_ref[other, cols] = ent_ref[other, cols] - (arrived(0, tile) + arrived(2, tile))

    def cf_copy(o):
        piece = cf.at[o]
        return remote(piece, piece, cf_sem, o - 1, (depth, core, o))

    def zero_copy(o):
        piece = cf.at[0]
        return remote(piece, piece, cf_sem, 6 + o, (depth, core, o))

    @pl.when(col == 0)
    def _():
        cf[...] = dot3(out_ref[:, :PW], inverse[...]).reshape(8, 48, PW)
        for o in range(1, 8):
            cf_copy(o).start()
        for o in range(1, 8):
            zero_copy(o).start()

    for tile in range(3):
        cols = slice(tile * 256, tile * 256 + 256)
        high, rest = split(top[:, :, :, :, :, cols].reshape(PW, 256))
        top_high[:, cols] = high
        top_low[:, cols] = rest

    @pl.when(col == 0)
    def _():
        for o in range(1, 8):
            cf_copy(o).wait_send()
            zero_copy(o).wait_send()

    def ring_copy(o, target):
        piece = cf.at[col]
        return remote(piece, piece, cg_sem, o - 1, (depth, core, target))

    for c in range(1, 8):

        @pl.when(col == c)
        def _():
            cf_copy(c).wait_recv()
            copies = []
            for o in range(1, 7):
                copy = ring_copy(o, (c - 1 + o) % 7 + 1)
                copy.start()
                copies.append(copy)
            zero_copy(c).wait_recv()
            for copy in copies:
                copy.wait()

    column = cf[...].reshape(384, PW)
    cf_ref[...] = column
    column_high, column_low = split(column)
    for tile in range(3):
        cols = slice(tile * 256, tile * 256 + 256)
        th, tl = top_high[:, cols], top_low[:, cols]
        out_ref[:, cols] = out_ref[:, cols] - (
            product(column_high, th) + (product(column_high, tl) + product(column_low, th))
        )

    for group in (
        *(sends for _, sends in stage1.values()), *stage2.values(), *passed.values(), *applied.values(),
        onward.values(), tops[0], tops[1], top_moves, gathers, [core_copy], moved,
    ):
        for copy in group:
            copy.wait_send()
    for q in range(6):
        for copy in own_copies(q):
            copy.wait_send()
    for g in range(3):
        for tile in range(3):
            for copy in other_copies(g, tile):
                copy.wait_send()
    entries(lambda copy: copy.wait_send())


def sems(count):
    return pltpu.SemaphoreType.DMA((2, count))


def local(lower_panels, upper_panels, given_inverse, structure, ancestor_entries):
    f32, bf16, i16 = jnp.float32, jnp.bfloat16, jnp.int16
    return pl.pallas_call(
        whole_kernel,
        name="whole",
        out_shape=(jax.ShapeDtypeStruct((384, PW), f32), jax.ShapeDtypeStruct((384, 768), f32)),
        in_specs=[pl.BlockSpec(memory_space=pltpu.SMEM)] + [VMEM] * 4,
        out_specs=(VMEM, VMEM),
        scratch_shapes=[
            pltpu.VMEM((2, 512, 768), bf16),
            pltpu.VMEM((8, 2, 2, 192, 128), bf16),
            pltpu.VMEM((2, 2, 128, 128), bf16),
            pltpu.VMEM((2, 3, 4, 2, 256, 256), bf16),
            pltpu.VMEM((8, 192, 2048), bf16),
            pltpu.VMEM((128, 2048), bf16),
            pltpu.VMEM((3, 2, 2, 3, 192, 256), i16),
            pltpu.VMEM((3, 2, 2, 3, 8, 256), f32),
            pltpu.VMEM((3, 2, 2, 3, 192, 256), i16),
            pltpu.VMEM((3, 2, 2, 3, 8, 256), f32),
            pltpu.VMEM((2, 3, 2, 192, 256), f32),
            pltpu.VMEM((3, 3, 192, 256), i16),
            pltpu.VMEM((3, 3, 8, 256), f32),
            pltpu.VMEM((3, 3, 192, 256), i16),
            pltpu.VMEM((3, 3, 8, 256), f32),
            pltpu.VMEM((2, 16, 768), f32),
            pltpu.VMEM((2, 4, 2, 16, 768), f32),
            pltpu.VMEM((3, 2, 2, 16, 768), f32),
            pltpu.VMEM((2, 2, 16, 768), f32),
            pltpu.VMEM((3, 16, 768), f32),
            pltpu.VMEM((2, 2, 4, 2, 16, 768), f32),
            pltpu.VMEM((PW, 768), bf16),
            pltpu.VMEM((PW, 768), bf16),
            pltpu.VMEM((PW, PW), f32),
            pltpu.VMEM((8, 48, PW), f32),
            sems(1), sems(27), pltpu.SemaphoreType.DMA((9,)), sems(18), sems(18), sems(3), sems(3), sems(3),
            sems(6), sems(6), sems(9), sems(9), sems(9), sems(9),
            sems(32), sems(6), sems(3), sems(7), sems(1), sems(14), sems(6),
        ],
        compiler_params=pltpu.CompilerParams(collective_id=0, has_side_effects=True, vmem_limit_bytes=LIMIT),
    )(structure, jnp.swapaxes(lower_panels, 2, 3), upper_panels, given_inverse, ancestor_entries)


def solution(mesh):
    return jax.shard_map(
        local,
        mesh=mesh,
        in_specs=(
            P("depth", None, None, ("rows", "cols")),
            P("depth", "rows", "cols"),
            P("depth", "rows", None),
            P("depth", None),
            P(("depth", "rows"), "cols"),
        ),
        out_specs=(P(("depth", "rows"), None), P(("depth", "rows"), "cols")),
        check_vma=False,
    )
```

```python
import functools

import jax
import jax.numpy as jnp
from jax import lax
from jax.experimental import pallas as pl
from jax.experimental.pallas import tpu as pltpu
from jax.sharding import PartitionSpec as P

PW = 512
MESH = pl.DeviceIdType.MESH
VMEM = pl.BlockSpec(memory_space=pltpu.VMEM)
LIMIT = 58 * 1024 * 1024
OFFSETS = (2, 1, 3, 0)
TOP = 32000.0


def place():
    depth, rows, cols = lax.axis_index("depth"), lax.axis_index("rows"), lax.axis_index("cols")
    return depth // 4, depth % 4, rows, cols // 2, cols % 2


def device(low, z, core, x, half):
    return (low * 4 + z, core, x * 2 + half)


def quantize(value, axis):
    most = jnp.maximum(jnp.max(jnp.abs(value), axis=axis, keepdims=True), 1e-30)
    return jnp.round(value * (TOP / most)).astype(jnp.int16), most / TOP


def split(value):
    high = value.astype(jnp.bfloat16)
    return high, (value - high.astype(jnp.float32)).astype(jnp.bfloat16)


def product(a, b):
    return jnp.dot(a, b, preferred_element_type=jnp.float32)


def dot3(a, b):
    (ah, al), (bh, bl) = split(a), split(b)
    return product(ah, bh) + (product(ah, bl) + product(al, bh))


def received(copies):
    for copy in copies:
        copy.wait_recv()


def whole_kernel(
    kept_ref, low_ref, up_ref, inv_ref, ent_ref, cf_ref, out_ref,
    up_other, turned, turned_top, app, lg, lg_top, cq, cs, rq, rs, own, sq, ss, tq, ts,
    ent_top, ctop, rtop, stop, ttop, top, top_high, top_low, inverse, cf,
    up_sem, l1_sem, loc_sem, l2_sem, f_sem, core_sem, half_sem, fwd_sem,
    r1_sem, r1s_sem, r1b_sem, r1bs_sem, r2_sem, r2s_sem,
    ent_sem, rt_sem, r2t_sem, tg_sem, tc_sem, cf_sem, cg_sem,
):
    low, z, core, x, half = place()
    depth, col = low * 4 + z, x * 2 + half

    def remote(src, dst, sems, index, target):
        return pltpu.make_async_remote_copy(
            src_ref=src, dst_ref=dst, send_sem=sems.at[0, index], recv_sem=sems.at[1, index],
            device_id=target, device_id_type=MESH,
        )

    partner = device(low, z, 1 - core, x, half)
    across = device(low, z, core, x, 1 - half)
    across_core = device(low, z, 1 - core, x, 1 - half)
    right = device(low, z, core, (x + 1) % 4, half)
    left = device(low, z, core, (x + 3) % 4, half)
    along_z = {o: device(low, (z + o) % 4, core, x, half) for o in (1, 2, 3)}
    along_y = [
        across,
        device(1 - low, z, core, x, half),
        device(1 - low, z, core, x, 1 - half),
    ]

    barrier = pltpu.get_barrier_semaphore()
    friends = [((depth + o // 2) % 8, core if o % 2 == 0 else 1 - core, col) for o in range(1, 16)]
    friends += [(depth, core, (col + o) % 8) for o in range(1, 8)]
    friends += [across_core, along_y[2]]
    for friend in friends:
        pl.semaphore_signal(barrier, inc=1, device_id=friend, device_id_type=MESH)
    upper_copy = remote(up_ref, up_other, up_sem, 0, partner)

    def entry_copy(g, row):
        target = ((g % 2) * 4 + (g // 2) % 4, g // 16, col)
        return pltpu.make_async_remote_copy(
            src_ref=ent_ref.at[pl.ds(pl.multiple_of(row * 16, 16), 16)], dst_ref=ent_top.at[(g // 8) % 2],
            send_sem=ent_sem.at[0, g], recv_sem=ent_sem.at[1, (g // 8) % 2],
            device_id=target, device_id_type=MESH,
        )

    holder = [(depth == 0) & (core == c) for c in range(2)]
    groups = ([g for g in range(24) if g not in (0, 8)], [g for g in range(25, 32)])
    stays = ([(0, 0), (8, 1)], [(24, 1)])

    def entries(act):
        for c in range(2):

            @pl.when(holder[c])
            def _():
                for g in groups[c]:
                    act(entry_copy(g, g - 24 * c))

    def wait_entries():
        @pl.when((depth != 0) | (core != 0))
        def _():
            for h in range(2):

                @pl.when((depth != 0) | (h == 0))
                def _():
                    pltpu.make_async_remote_copy(
                        src_ref=ent_ref.at[pl.ds(0, 16)], dst_ref=ent_top.at[h],
                        send_sem=ent_sem.at[0, 0], recv_sem=ent_sem.at[1, h],
                        device_id=partner, device_id_type=MESH,
                    ).wait_recv()

    def factor(s, block):
        return jnp.full((1, 128), kept_ref[s, block].astype(jnp.float32), jnp.float32)

    lane = pl.multiple_of((x * 4 + core * 2 + half) * 128, 128)
    sharers = ((across, core, 1 - half), (across_core, 1 - core, 1 - half), (partner, 1 - core, half))

    def turn_over(j, part):
        lanes = slice(part * 128, part * 128 + 128)
        both = jnp.concatenate(
            [low_ref[s, j, :, lanes] * factor(s, j * 6 + part).astype(jnp.bfloat16) for s in range(2)]
        )
        return both.T

    def share(src, dst, first):
        here = pltpu.make_async_copy(src(core, half), dst, loc_sem.at[first // 3])
        here.start()
        sends = []
        for t, (target, r, h) in enumerate(sharers):
            copy = remote(src(r, h), dst, l1_sem, first + t, target)
            copy.start()
            sends.append(copy)
        return here, sends

    def turn_top():
        for part in range(4):
            turned_top[part // 2, part % 2] = turn_over(0, part)

    def share_top():
        return share(lambda r, h: turned_top.at[r, h], lg_top.at[:, pl.ds(lane, 128)], 24)

    def turn_rows(q):
        j = (q % 2) * 4 + (z + OFFSETS[q // 2]) % 4
        for part in range(6):
            value = turn_over(j, part)
            for piece in range(2):
                row = part * 128 + piece * 64
                turned[q, row // 384, (row // 192) % 2, row % 192:row % 192 + 64] = (
                    value[piece * 64:piece * 64 + 64]
                )

    def share_rows(q):
        return share(lambda r, h: turned.at[q, r, h], lg.at[q, :, pl.ds(lane, 128)], q * 3)

    mine, theirs = pl.multiple_of(core * 512, 512), pl.multiple_of((1 - core) * 512, 512)

    def apply(tile):
        cols = slice(tile * 256, tile * 256 + 256)
        for s in range(2):
            total = product(inv_ref[s, :, pl.ds(mine, 512)], up_ref[s, :, cols]) + product(
                inv_ref[s, :, pl.ds(theirs, 512)], up_other[s, :, cols]
            )
            block = col * 6 + tile * 2
            mask = jnp.concatenate([factor(s, block), factor(s, block + 1)], axis=1)
            applied = (total * mask).astype(jnp.bfloat16)
            for c in range(8):
                app[half, tile, c // 2, core, (c % 2) * 128 + s * 64:(c % 2) * 128 + s * 64 + 64] = (
                    applied[c * 64:(c + 1) * 64]
                )
        part = app.at[half, tile, :, core]
        copies = [remote(part, part, core_sem, tile, partner), remote(part, part, half_sem, tile, across)]
        copies[0].start()
        return copies

    def forward_applied(tile):
        part = app.at[1 - half, tile, :, core]
        copy = remote(part, part, fwd_sem, tile, partner)
        copy.start()
        return copy

    at_home = pl.ds(pl.multiple_of(x * 512, 512), 512)
    from_left = pl.ds(pl.multiple_of(((x + 3) % 4) * 512, 512), 512)
    from_right = pl.ds(pl.multiple_of(((x + 1) % 4) * 512, 512), 512)

    def both_ways(first, second, sems, q):
        copies = [remote(first, first, sems, q * 2, right), remote(second, second, sems, q * 2 + 1, left)]
        for copy in copies:
            copy.start()
        return copies

    def rows_of(q):
        return (lg_top, 64) if q == 8 else (lg.at[q], 96)

    def ring(q):
        block = rows_of(q)[0].at[:, at_home]
        return both_ways(block, block, l2_sem, q)

    def forward(q):
        rows, count = rows_of(q)
        return both_ways(
            rows.at[pl.ds(0, count), from_left], rows.at[pl.ds(count, count), from_right], f_sem, q
        )

    sides = (half, 1 - half)

    def own_copies(q):
        o, b = OFFSETS[q // 2], q % 2
        return (
            remote(cq.at[o - 1, b, 0], rq.at[o - 1, b, 0], r1_sem, q, along_z[o]),
            remote(cs.at[o - 1, b, 0], rs.at[o - 1, b, 0], r1s_sem, q, along_z[o]),
        )

    def give_own(q):
        o, b = OFFSETS[q // 2], q % 2

        @pl.loop(0, 3)
        def _(tile):
            total = product(lg[q], app[half, tile].reshape(2048, 256))
            if o == 0:
                own[0, tile, b] = total
            else:
                values, scale = quantize(total, 0)
                cq[o - 1, b, 0, tile] = values
                cs[o - 1, b, 0, tile] = jnp.broadcast_to(scale, (8, 256))

        if o != 0:
            for copy in own_copies(q):
                copy.start()

    def other_copies(g, tile):
        o = OFFSETS[g]
        return (
            remote(cq.at[o - 1, :, 1, tile], rq.at[o - 1, :, 1, tile], r1b_sem, g * 3 + tile, along_z[o]),
            remote(cs.at[o - 1, :, 1, tile], rs.at[o - 1, :, 1, tile], r1bs_sem, g * 3 + tile, along_z[o]),
        )

    def give_other(g, tile):
        o = OFFSETS[g]
        total = product(
            lg[g * 2:g * 2 + 2].reshape(384, 2048), app[1 - half, tile].reshape(2048, 256)
        ).reshape(2, 192, 256)
        if o == 0:
            own[1, tile] = total
            return
        values, scale = quantize(total, 1)
        for b in range(2):
            cq[o - 1, b, 1, tile] = values[b]
            cs[o - 1, b, 1, tile] = jnp.broadcast_to(scale[b], (8, 256))
        for copy in other_copies(g, tile):
            copy.start()

    def make_top(turn, tile):
        total = product(lg_top[...], app[sides[turn], tile].reshape(2048, 256))
        ctop[turn, :, :, :, tile * 256:tile * 256 + 256] = total.reshape(4, 2, 16, 256)

    def top_copies(turn):
        return [
            remote(ctop.at[turn, (z + o) % 4], rtop.at[o - 1, turn], rt_sem, turn * 3 + o - 1, along_z[o])
            for o in (1, 2, 3)
        ]

    def give_top(turn):
        copies = top_copies(turn)
        for copy in copies:
            copy.start()
        return copies

    stage1, stage2, passed, applied, onward, tops = {}, {}, {}, {}, {}, {}

    def start_ring(q):
        stage1[q][0].wait()
        received(stage1[q][1])
        stage2[q] = ring(q)

    turn_top()
    turn_rows(0)
    pl.semaphore_wait(barrier, len(friends))
    stage1[8] = share_top()
    stage1[0] = share_rows(0)
    upper_copy.start()
    for q in range(1, 4):
        turn_rows(q)
        stage1[q] = share_rows(q)
    start_ring(8)
    start_ring(0)
    entries(lambda copy: copy.start())
    for c in range(2):

        @pl.when(holder[c])
        def _():
            for g, h in stays[c]:
                row = (g - 24 * c) * 16
                ent_top[h] = ent_ref[row:row + 16, :]

    upper_copy.wait()
    applied[0] = apply(0)
    start_ring(1)
    for q in range(4, 8):
        turn_rows(q)
        stage1[q] = share_rows(q)
    applied[0][1].start()
    received(stage2[8])
    passed[8] = forward(8)
    applied[1] = apply(1)
    applied[2] = apply(2)

    for q in range(8):
        received(stage2[q])
        passed[q] = forward(q)
        if q + 2 < 8:
            start_ring(q + 2)
        if q == 0:
            applied[1][1].start()
            received([applied[t][0] for t in range(3)])
            received(passed[8])
            for tile in range(3):
                make_top(0, tile)
            tops[0] = give_top(0)
        else:
            received(passed[q - 1])
            give_own(q - 1)
        if q in (2, 4, 6):
            tile = q // 2 - 1
            applied[tile][1].wait_recv()
            onward[tile] = forward_applied(tile)
        if q == 2:
            applied[2][1].start()
        if q in (3, 5, 7):
            onward[q // 2 - 1].wait_recv()
            make_top(1, q // 2 - 1)
        if q == 3:
            give_other(0, 0)
        if q == 4:
            give_other(1, 0)
        if q == 5:
            give_other(0, 1)
            give_other(1, 1)
        if q == 6:
            give_other(2, 0)
            give_other(2, 1)
        if q == 7:
            tops[1] = give_top(1)
            for g in range(3):
                give_other(g, 2)
    received(passed[7])
    give_own(7)

    received(tops[0])
    received(tops[1])
    for turn in range(2):
        total = ctop[turn, z]
        for o in range(3):
            total = total + rtop[o, turn]
        stop[turn] = total
    top_moves = [
        remote(stop.at[turn, row], ttop.at[t], r2t_sem, t, along_y[t])
        for t, (turn, row) in enumerate(((1, low), (0, 1 - low), (1, 1 - low)))
    ]
    for copy in top_moves:
        copy.start()
    for tile in range(3):
        give_other(3, tile)

    def chunk_sum(turn, row, tile):
        total = own[turn, tile, row]
        for o in range(3):
            total = total + rq[o, row, turn, tile].astype(jnp.float32) * rs[o, row, turn, tile, 0:1, :]
        return total

    moved = []

    def hand(t, turn, row, tile):
        values, scale = quantize(chunk_sum(turn, row, tile), 0)
        sq[t, tile] = values
        ss[t, tile] = jnp.broadcast_to(scale, (8, 256))
        copies = [
            remote(sq.at[t, tile], tq.at[t, tile], r2_sem, t * 3 + tile, along_y[t]),
            remote(ss.at[t, tile], ts.at[t, tile], r2s_sem, t * 3 + tile, along_y[t]),
        ]
        for copy in copies:
            copy.start()
        moved.extend(copies)

    for q in range(6):
        received(own_copies(q))
    for tile in range(3):
        hand(1, 0, 1 - low, tile)

    received(top_moves)
    wait_entries()

    top[core, half, z, low] = ent_top[half] - (stop[0, low] + ttop[1])
    top[core, 1 - half, z, low] = ent_top[1 - half] - (ttop[0] + ttop[2])
    gathers = []
    for o in range(1, 8):
        piece = top.at[core, :, z, low]
        copy = remote(piece, piece, tg_sem, o - 1, ((depth + o) % 8, core, col))
        copy.start()
        gathers.append(copy)

    for tile in range(3):
        for g in range(3):
            received(other_copies(g, tile))
        hand(0, 1, low, tile)
        hand(2, 1, 1 - low, tile)
        if tile == 0:
            received(gathers)
            core_copy = remote(top.at[core], top.at[core], tc_sem, 0, partner)
            core_copy.start()
    core_copy.wait_recv()

    @pl.when(col == 0)
    def _():
        row = lax.broadcasted_iota(jnp.int32, (PW, PW), 0)
        identity = (row == lax.broadcasted_iota(jnp.int32, (PW, PW), 1)).astype(jnp.float32)
        pivot = top[:, :, :, :, :, :PW].reshape(PW, PW)
        error = identity - pivot * (1.0 / 16.0)
        square = dot3(error, error)
        inverse[...] = dot3(identity + error, identity + square) * (1.0 / 16.0)

    def arrived(t, tile):
        return tq[t, tile].astype(jnp.float32) * ts[t, tile, 0:1, :]

    mine = pl.ds(pl.multiple_of(half * 192, 192), 192)
    other = pl.ds(pl.multiple_of((1 - half) * 192, 192), 192)
    received(moved[0:6])
    for tile in range(3):
        cols = slice(tile * 256, tile * 256 + 256)
        out_ref[mine, cols] = ent_ref[mine, cols] - (chunk_sum(0, low, tile) + arrived(1, tile))
    for tile in range(3):
        received(moved[6 + tile * 4:10 + tile * 4])
        cols = slice(tile * 256, tile * 256 + 256)
        out_ref[other, cols] = ent_ref[other, cols] - (arrived(0, tile) + arrived(2, tile))

    def piece(c):
        return cf.at[(c - 1) * 56:min(c * 56, 384)]

    def cf_copy(c):
        return remote(piece(c), piece(c), cf_sem, c - 1, (depth, core, c))

    def hand_on(c, target):
        return pltpu.make_async_remote_copy(
            src_ref=piece(c), dst_ref=piece(c), send_sem=cg_sem.at[0, target - 1], recv_sem=cg_sem.at[1, c - 1],
            device_id=(depth, core, target), device_id_type=MESH,
        )

    @pl.when(col == 0)
    def _():
        cf[...] = dot3(out_ref[:, :PW], inverse[...])
        for c in (4, 5, 2, 3, 6, 7, 1):
            cf_copy(c).start()

    for tile in range(3):
        cols = slice(tile * 256, tile * 256 + 256)
        high, rest = split(top[:, :, :, :, :, cols].reshape(PW, 256))
        top_high[:, cols] = high
        top_low[:, cols] = rest

    @pl.when(col == 0)
    def _():
        for c in range(1, 8):
            cf_copy(c).wait_send()

    for c in range(1, 8):

        @pl.when(col == c)
        def _():
            cf_copy(c).wait_recv()
            others = [k for k in range(1, 8) if k != c]
            copies = [hand_on(c, k) for k in others]
            for copy in copies:
                copy.start()
            for k in others:
                hand_on(k, k).wait_recv()
            for copy in copies:
                copy.wait_send()

    column = cf[...]
    cf_ref[...] = column
    column_high, column_low = split(column)
    for tile in range(3):
        cols = slice(tile * 256, tile * 256 + 256)
        th, tl = top_high[:, cols], top_low[:, cols]
        out_ref[:, cols] = out_ref[:, cols] - (
            product(column_high, th) + (product(column_high, tl) + product(column_low, th))
        )

    for group in (
        *(sends for _, sends in stage1.values()), *stage2.values(), *passed.values(), *applied.values(),
        onward.values(), tops[0], tops[1], top_moves, gathers, [core_copy], moved,
    ):
        for copy in group:
            copy.wait_send()
    for q in range(6):
        for copy in own_copies(q):
            copy.wait_send()
    for g in range(3):
        for tile in range(3):
            for copy in other_copies(g, tile):
                copy.wait_send()
    entries(lambda copy: copy.wait_send())


def sems(count):
    return pltpu.SemaphoreType.DMA((2, count))


def local(lower_panels, upper_panels, given_inverse, structure, ancestor_entries):
    f32, bf16, i16 = jnp.float32, jnp.bfloat16, jnp.int16
    return pl.pallas_call(
        whole_kernel,
        name="whole",
        out_shape=(jax.ShapeDtypeStruct((384, PW), f32), jax.ShapeDtypeStruct((384, 768), f32)),
        in_specs=[pl.BlockSpec(memory_space=pltpu.SMEM)] + [VMEM] * 4,
        out_specs=(VMEM, VMEM),
        scratch_shapes=[
            pltpu.VMEM((2, 512, 768), bf16),
            pltpu.VMEM((8, 2, 2, 192, 128), bf16),
            pltpu.VMEM((2, 2, 128, 128), bf16),
            pltpu.VMEM((2, 3, 4, 2, 256, 256), bf16),
            pltpu.VMEM((8, 192, 2048), bf16),
            pltpu.VMEM((128, 2048), bf16),
            pltpu.VMEM((3, 2, 2, 3, 192, 256), i16),
            pltpu.VMEM((3, 2, 2, 3, 8, 256), f32),
            pltpu.VMEM((3, 2, 2, 3, 192, 256), i16),
            pltpu.VMEM((3, 2, 2, 3, 8, 256), f32),
            pltpu.VMEM((2, 3, 2, 192, 256), f32),
            pltpu.VMEM((3, 3, 192, 256), i16),
            pltpu.VMEM((3, 3, 8, 256), f32),
            pltpu.VMEM((3, 3, 192, 256), i16),
            pltpu.VMEM((3, 3, 8, 256), f32),
            pltpu.VMEM((2, 16, 768), f32),
            pltpu.VMEM((2, 4, 2, 16, 768), f32),
            pltpu.VMEM((3, 2, 2, 16, 768), f32),
            pltpu.VMEM((2, 2, 16, 768), f32),
            pltpu.VMEM((3, 16, 768), f32),
            pltpu.VMEM((2, 2, 4, 2, 16, 768), f32),
            pltpu.VMEM((PW, 768), bf16),
            pltpu.VMEM((PW, 768), bf16),
            pltpu.VMEM((PW, PW), f32),
            pltpu.VMEM((384, PW), f32),
            sems(1), sems(27), pltpu.SemaphoreType.DMA((9,)), sems(18), sems(18), sems(3), sems(3), sems(3),
            sems(6), sems(6), sems(9), sems(9), sems(9), sems(9),
            sems(32), sems(6), sems(3), sems(7), sems(1), sems(7), sems(14),
        ],
        compiler_params=pltpu.CompilerParams(collective_id=0, has_side_effects=True, vmem_limit_bytes=LIMIT),
    )(structure, jnp.swapaxes(lower_panels, 2, 3), upper_panels, given_inverse, ancestor_entries)


def solution(mesh):
    return jax.shard_map(
        local,
        mesh=mesh,
        in_specs=(
            P("depth", None, None, ("rows", "cols")),
            P("depth", "rows", "cols"),
            P("depth", "rows", None),
            P("depth", None),
            P(("depth", "rows"), "cols"),
        ),
        out_specs=(P(("depth", "rows"), None), P(("depth", "rows"), "cols")),
        check_vma=False,
    )
```

```python
import functools

import jax
import jax.numpy as jnp
from jax import lax
from jax.experimental import pallas as pl
from jax.experimental.pallas import tpu as pltpu
from jax.sharding import PartitionSpec as P

PW = 512
MESH = pl.DeviceIdType.MESH
VMEM = pl.BlockSpec(memory_space=pltpu.VMEM)
LIMIT = 58 * 1024 * 1024
OFFSETS = (2, 1, 3, 0)
TOP = 32000.0


def place():
    depth, rows, cols = lax.axis_index("depth"), lax.axis_index("rows"), lax.axis_index("cols")
    return depth // 4, depth % 4, rows, cols // 2, cols % 2


def device(low, z, core, x, half):
    return (low * 4 + z, core, x * 2 + half)


def quantize(value, axis):
    most = jnp.maximum(jnp.max(jnp.abs(value), axis=axis, keepdims=True), 1e-30)
    return jnp.round(value * (TOP / most)).astype(jnp.int16), most / TOP


def split(value):
    high = value.astype(jnp.bfloat16)
    return high, (value - high.astype(jnp.float32)).astype(jnp.bfloat16)


def product(a, b):
    return jnp.dot(a, b, preferred_element_type=jnp.float32)


def dot3(a, b):
    (ah, al), (bh, bl) = split(a), split(b)
    return product(ah, bh) + (product(ah, bl) + product(al, bh))


def received(copies):
    for copy in copies:
        copy.wait_recv()


def whole_kernel(
    kept_ref, low_ref, up_ref, inv_ref, ent_ref, cf_ref, out_ref,
    up_other, turned, turned_top, app, lg, lg_top, cq, cs, rq, rs, own, sq, ss, tq, ts,
    ent_top, ctop, rtop, stop, ttop, top, top_high, top_low, inverse, cf, cf_scale,
    up_sem, l1_sem, loc_sem, l2_sem, f_sem, core_sem, half_sem, fwd_sem,
    r1_sem, r1s_sem, r1b_sem, r1bs_sem, r2_sem, r2s_sem,
    ent_sem, rt_sem, r2t_sem, tg_sem, tc_sem, cf_sem, cfs_sem, cg_sem,
):
    low, z, core, x, half = place()
    depth, col = low * 4 + z, x * 2 + half

    def remote(src, dst, sems, index, target):
        return pltpu.make_async_remote_copy(
            src_ref=src, dst_ref=dst, send_sem=sems.at[0, index], recv_sem=sems.at[1, index],
            device_id=target, device_id_type=MESH,
        )

    partner = device(low, z, 1 - core, x, half)
    across = device(low, z, core, x, 1 - half)
    across_core = device(low, z, 1 - core, x, 1 - half)
    right = device(low, z, core, (x + 1) % 4, half)
    left = device(low, z, core, (x + 3) % 4, half)
    along_z = {o: device(low, (z + o) % 4, core, x, half) for o in (1, 2, 3)}
    along_y = [
        across,
        device(1 - low, z, core, x, half),
        device(1 - low, z, core, x, 1 - half),
    ]

    barrier = pltpu.get_barrier_semaphore()
    friends = [((depth + o // 2) % 8, core if o % 2 == 0 else 1 - core, col) for o in range(1, 16)]
    friends += [(depth, core, (col + o) % 8) for o in range(1, 8)]
    friends += [across_core, along_y[2]]
    for friend in friends:
        pl.semaphore_signal(barrier, inc=1, device_id=friend, device_id_type=MESH)
    upper_copy = remote(up_ref, up_other, up_sem, 0, partner)

    def entry_copy(g, row):
        target = ((g % 2) * 4 + (g // 2) % 4, g // 16, col)
        return pltpu.make_async_remote_copy(
            src_ref=ent_ref.at[pl.ds(pl.multiple_of(row * 16, 16), 16)], dst_ref=ent_top.at[(g // 8) % 2],
            send_sem=ent_sem.at[0, g], recv_sem=ent_sem.at[1, (g // 8) % 2],
            device_id=target, device_id_type=MESH,
        )

    holder = [(depth == 0) & (core == c) for c in range(2)]
    groups = ([g for g in range(24) if g not in (0, 8)], [g for g in range(25, 32)])
    stays = ([(0, 0), (8, 1)], [(24, 1)])

    def entries(act):
        for c in range(2):

            @pl.when(holder[c])
            def _():
                for g in groups[c]:
                    act(entry_copy(g, g - 24 * c))

    def wait_entries():
        @pl.when((depth != 0) | (core != 0))
        def _():
            for h in range(2):

                @pl.when((depth != 0) | (h == 0))
                def _():
                    pltpu.make_async_remote_copy(
                        src_ref=ent_ref.at[pl.ds(0, 16)], dst_ref=ent_top.at[h],
                        send_sem=ent_sem.at[0, 0], recv_sem=ent_sem.at[1, h],
                        device_id=partner, device_id_type=MESH,
                    ).wait_recv()

    def factor(s, block):
        return jnp.full((1, 128), kept_ref[s, block].astype(jnp.float32), jnp.float32)

    lane = pl.multiple_of((x * 4 + core * 2 + half) * 128, 128)
    sharers = ((across, core, 1 - half), (across_core, 1 - core, 1 - half), (partner, 1 - core, half))

    def turn_over(j, part):
        lanes = slice(part * 128, part * 128 + 128)
        both = jnp.concatenate(
            [low_ref[s, j, :, lanes] * factor(s, j * 6 + part).astype(jnp.bfloat16) for s in range(2)]
        )
        return both.T

    def share(src, dst, first):
        here = pltpu.make_async_copy(src(core, half), dst, loc_sem.at[first // 3])
        here.start()
        sends = []
        for t, (target, r, h) in enumerate(sharers):
            copy = remote(src(r, h), dst, l1_sem, first + t, target)
            copy.start()
            sends.append(copy)
        return here, sends

    def turn_top():
        for part in range(4):
            turned_top[part // 2, part % 2] = turn_over(0, part)

    def share_top():
        return share(lambda r, h: turned_top.at[r, h], lg_top.at[:, pl.ds(lane, 128)], 24)

    def turn_rows(q):
        j = (q % 2) * 4 + (z + OFFSETS[q // 2]) % 4
        for part in range(6):
            value = turn_over(j, part)
            for piece in range(2):
                row = part * 128 + piece * 64
                turned[q, row // 384, (row // 192) % 2, row % 192:row % 192 + 64] = (
                    value[piece * 64:piece * 64 + 64]
                )

    def share_rows(q):
        return share(lambda r, h: turned.at[q, r, h], lg.at[q, :, pl.ds(lane, 128)], q * 3)

    mine, theirs = pl.multiple_of(core * 512, 512), pl.multiple_of((1 - core) * 512, 512)

    def apply(tile):
        cols = slice(tile * 256, tile * 256 + 256)
        for s in range(2):
            total = product(inv_ref[s, :, pl.ds(mine, 512)], up_ref[s, :, cols]) + product(
                inv_ref[s, :, pl.ds(theirs, 512)], up_other[s, :, cols]
            )
            block = col * 6 + tile * 2
            mask = jnp.concatenate([factor(s, block), factor(s, block + 1)], axis=1)
            applied = (total * mask).astype(jnp.bfloat16)
            for c in range(8):
                app[half, tile, c // 2, core, (c % 2) * 128 + s * 64:(c % 2) * 128 + s * 64 + 64] = (
                    applied[c * 64:(c + 1) * 64]
                )
        part = app.at[half, tile, :, core]
        copies = [remote(part, part, core_sem, tile, partner), remote(part, part, half_sem, tile, across)]
        copies[0].start()
        return copies

    def forward_applied(tile):
        part = app.at[1 - half, tile, :, core]
        copy = remote(part, part, fwd_sem, tile, partner)
        copy.start()
        return copy

    at_home = pl.ds(pl.multiple_of(x * 512, 512), 512)
    from_left = pl.ds(pl.multiple_of(((x + 3) % 4) * 512, 512), 512)
    from_right = pl.ds(pl.multiple_of(((x + 1) % 4) * 512, 512), 512)

    def both_ways(first, second, sems, q):
        copies = [remote(first, first, sems, q * 2, right), remote(second, second, sems, q * 2 + 1, left)]
        for copy in copies:
            copy.start()
        return copies

    def rows_of(q):
        return (lg_top, 64) if q == 8 else (lg.at[q], 96)

    def ring(q):
        block = rows_of(q)[0].at[:, at_home]
        return both_ways(block, block, l2_sem, q)

    def forward(q):
        rows, count = rows_of(q)
        return both_ways(
            rows.at[pl.ds(0, count), from_left], rows.at[pl.ds(count, count), from_right], f_sem, q
        )

    sides = (half, 1 - half)

    def own_copies(q):
        o, b = OFFSETS[q // 2], q % 2
        return (
            remote(cq.at[o - 1, b, 0], rq.at[o - 1, b, 0], r1_sem, q, along_z[o]),
            remote(cs.at[o - 1, b, 0], rs.at[o - 1, b, 0], r1s_sem, q, along_z[o]),
        )

    def give_own(q):
        o, b = OFFSETS[q // 2], q % 2

        @pl.loop(0, 3)
        def _(tile):
            total = product(lg[q], app[half, tile].reshape(2048, 256))
            if o == 0:
                own[0, tile, b] = total
            else:
                values, scale = quantize(total, 0)
                cq[o - 1, b, 0, tile] = values
                cs[o - 1, b, 0, tile] = jnp.broadcast_to(scale, (8, 256))

        if o != 0:
            for copy in own_copies(q):
                copy.start()

    def other_copies(g, tile):
        o = OFFSETS[g]
        return (
            remote(cq.at[o - 1, :, 1, tile], rq.at[o - 1, :, 1, tile], r1b_sem, g * 3 + tile, along_z[o]),
            remote(cs.at[o - 1, :, 1, tile], rs.at[o - 1, :, 1, tile], r1bs_sem, g * 3 + tile, along_z[o]),
        )

    def give_other(g, tile):
        o = OFFSETS[g]
        total = product(
            lg[g * 2:g * 2 + 2].reshape(384, 2048), app[1 - half, tile].reshape(2048, 256)
        ).reshape(2, 192, 256)
        if o == 0:
            own[1, tile] = total
            return
        values, scale = quantize(total, 1)
        for b in range(2):
            cq[o - 1, b, 1, tile] = values[b]
            cs[o - 1, b, 1, tile] = jnp.broadcast_to(scale[b], (8, 256))
        for copy in other_copies(g, tile):
            copy.start()

    def make_top(turn, tile):
        total = product(lg_top[...], app[sides[turn], tile].reshape(2048, 256))
        ctop[turn, :, :, :, tile * 256:tile * 256 + 256] = total.reshape(4, 2, 16, 256)

    def top_copies(turn):
        return [
            remote(ctop.at[turn, (z + o) % 4], rtop.at[o - 1, turn], rt_sem, turn * 3 + o - 1, along_z[o])
            for o in (1, 2, 3)
        ]

    def give_top(turn):
        copies = top_copies(turn)
        for copy in copies:
            copy.start()
        return copies

    stage1, stage2, passed, applied, onward, tops = {}, {}, {}, {}, {}, {}

    def start_ring(q):
        stage1[q][0].wait()
        received(stage1[q][1])
        stage2[q] = ring(q)

    turn_top()
    turn_rows(0)
    pl.semaphore_wait(barrier, len(friends))
    stage1[8] = share_top()
    stage1[0] = share_rows(0)
    upper_copy.start()
    for q in range(1, 4):
        turn_rows(q)
        stage1[q] = share_rows(q)
    start_ring(8)
    start_ring(0)
    entries(lambda copy: copy.start())
    for c in range(2):

        @pl.when(holder[c])
        def _():
            for g, h in stays[c]:
                row = (g - 24 * c) * 16
                ent_top[h] = ent_ref[row:row + 16, :]

    upper_copy.wait()
    applied[0] = apply(0)
    start_ring(1)
    for q in range(4, 8):
        turn_rows(q)
        stage1[q] = share_rows(q)
    applied[0][1].start()
    received(stage2[8])
    passed[8] = forward(8)
    applied[1] = apply(1)
    applied[2] = apply(2)

    for q in range(8):
        received(stage2[q])
        passed[q] = forward(q)
        if q + 2 < 8:
            start_ring(q + 2)
        if q == 0:
            applied[1][1].start()
            received([applied[t][0] for t in range(3)])
            received(passed[8])
            for tile in range(3):
                make_top(0, tile)
            tops[0] = give_top(0)
        else:
            received(passed[q - 1])
            give_own(q - 1)
        if q in (2, 4, 6):
            tile = q // 2 - 1
            applied[tile][1].wait_recv()
            onward[tile] = forward_applied(tile)
        if q == 2:
            applied[2][1].start()
        if q in (3, 5, 7):
            onward[q // 2 - 1].wait_recv()
            make_top(1, q // 2 - 1)
        if q == 3:
            give_other(0, 0)
        if q == 4:
            give_other(1, 0)
        if q == 5:
            give_other(0, 1)
            give_other(1, 1)
        if q == 6:
            give_other(2, 0)
            give_other(2, 1)
        if q == 7:
            tops[1] = give_top(1)
            for g in range(3):
                give_other(g, 2)
    received(passed[7])
    give_own(7)

    received(tops[0])
    received(tops[1])
    for turn in range(2):
        total = ctop[turn, z]
        for o in range(3):
            total = total + rtop[o, turn]
        stop[turn] = total
    top_moves = [
        remote(stop.at[turn, row], ttop.at[t], r2t_sem, t, along_y[t])
        for t, (turn, row) in enumerate(((1, low), (0, 1 - low), (1, 1 - low)))
    ]
    for copy in top_moves:
        copy.start()
    for tile in range(3):
        give_other(3, tile)

    def chunk_sum(turn, row, tile):
        total = own[turn, tile, row]
        for o in range(3):
            total = total + rq[o, row, turn, tile].astype(jnp.float32) * rs[o, row, turn, tile, 0:1, :]
        return total

    moved = []

    def hand(t, turn, row, tile):
        values, scale = quantize(chunk_sum(turn, row, tile), 0)
        sq[t, tile] = values
        ss[t, tile] = jnp.broadcast_to(scale, (8, 256))
        copies = [
            remote(sq.at[t, tile], tq.at[t, tile], r2_sem, t * 3 + tile, along_y[t]),
            remote(ss.at[t, tile], ts.at[t, tile], r2s_sem, t * 3 + tile, along_y[t]),
        ]
        for copy in copies:
            copy.start()
        moved.extend(copies)

    for q in range(6):
        received(own_copies(q))
    for tile in range(3):
        hand(1, 0, 1 - low, tile)

    received(top_moves)
    wait_entries()

    top[core, half, z, low] = ent_top[half] - (stop[0, low] + ttop[1])
    top[core, 1 - half, z, low] = ent_top[1 - half] - (ttop[0] + ttop[2])
    gathers = []
    for o in range(1, 8):
        piece = top.at[core, :, z, low]
        copy = remote(piece, piece, tg_sem, o - 1, ((depth + o) % 8, core, col))
        copy.start()
        gathers.append(copy)

    for tile in range(3):
        for g in range(3):
            received(other_copies(g, tile))
        hand(0, 1, low, tile)
        hand(2, 1, 1 - low, tile)
    received(gathers)
    core_copy = remote(top.at[core], top.at[core], tc_sem, 0, partner)
    core_copy.start()

    def arrived(t, tile):
        return tq[t, tile].astype(jnp.float32) * ts[t, tile, 0:1, :]

    mine = pl.ds(pl.multiple_of(half * 192, 192), 192)
    other = pl.ds(pl.multiple_of((1 - half) * 192, 192), 192)
    received(moved[0:6])
    for tile in range(3):
        cols = slice(tile * 256, tile * 256 + 256)
        out_ref[mine, cols] = ent_ref[mine, cols] - (chunk_sum(0, low, tile) + arrived(1, tile))
    for tile in range(3):
        received(moved[6 + tile * 4:10 + tile * 4])
        cols = slice(tile * 256, tile * 256 + 256)
        out_ref[other, cols] = ent_ref[other, cols] - (arrived(0, tile) + arrived(2, tile))

    core_copy.wait_recv()

    @pl.when(col == 0)
    def _():
        row = lax.broadcasted_iota(jnp.int32, (PW, PW), 0)
        identity = (row == lax.broadcasted_iota(jnp.int32, (PW, PW), 1)).astype(jnp.float32)
        pivot = top[:, :, :, :, :, :PW].reshape(PW, PW)
        error = identity - pivot * (1.0 / 16.0)
        square = dot3(error, error)
        inverse[...] = dot3(identity + error, identity + square) * (1.0 / 16.0)

    bounds = (0, 64, 128, 192, 240, 288, 336, 384)

    def piece(c):
        return cf.at[bounds[c - 1]:bounds[c]]

    def scale_copy(c):
        return remote(cf_scale, cf_scale, cfs_sem, c - 1, (depth, core, c))

    first_row = depth * 768 + core * 384
    unit = (
        lax.broadcasted_iota(jnp.int32, (384, PW), 0) + first_row == lax.broadcasted_iota(jnp.int32, (384, PW), 1)
    ).astype(jnp.float32)

    def cf_copy(c):
        return remote(piece(c), piece(c), cf_sem, c - 1, (depth, core, c))

    def hand_on(c, target):
        return pltpu.make_async_remote_copy(
            src_ref=piece(c), dst_ref=piece(c), send_sem=cg_sem.at[0, target - 1], recv_sem=cg_sem.at[1, c - 1],
            device_id=(depth, core, target), device_id_type=MESH,
        )

    @pl.when(col == 0)
    def _():
        values, scale = quantize(dot3(out_ref[:, :PW], inverse[...]) - unit, 0)
        cf[...] = values
        cf_scale[...] = jnp.broadcast_to(scale, (8, PW))
        for c in (4, 5, 2, 3, 6, 7, 1):
            cf_copy(c).start()
        for c in range(1, 8):
            scale_copy(c).start()

    for tile in range(3):
        cols = slice(tile * 256, tile * 256 + 256)
        high, rest = split(top[:, :, :, :, :, cols].reshape(PW, 256))
        top_high[:, cols] = high
        top_low[:, cols] = rest

    @pl.when(col == 0)
    def _():
        for c in range(1, 8):
            cf_copy(c).wait_send()
            scale_copy(c).wait_send()

    for c in range(1, 8):

        @pl.when(col == c)
        def _():
            cf_copy(c).wait_recv()
            others = [k for k in range(1, 8) if k != c]
            copies = [hand_on(c, k) for k in others]
            for copy in copies:
                copy.start()
            for k in others:
                hand_on(k, k).wait_recv()
            scale_copy(c).wait_recv()
            for copy in copies:
                copy.wait_send()

    column = cf[...].astype(jnp.float32) * cf_scale[0:1, :] + unit
    cf_ref[...] = column
    column_high, column_low = split(column)
    for tile in range(3):
        cols = slice(tile * 256, tile * 256 + 256)
        th, tl = top_high[:, cols], top_low[:, cols]
        out_ref[:, cols] = out_ref[:, cols] - (
            product(column_high, th) + (product(column_high, tl) + product(column_low, th))
        )

    for group in (
        *(sends for _, sends in stage1.values()), *stage2.values(), *passed.values(), *applied.values(),
        onward.values(), tops[0], tops[1], top_moves, gathers, [core_copy], moved,
    ):
        for copy in group:
            copy.wait_send()
    for q in range(6):
        for copy in own_copies(q):
            copy.wait_send()
    for g in range(3):
        for tile in range(3):
            for copy in other_copies(g, tile):
                copy.wait_send()
    entries(lambda copy: copy.wait_send())


def sems(count):
    return pltpu.SemaphoreType.DMA((2, count))


def local(lower_panels, upper_panels, given_inverse, structure, ancestor_entries):
    f32, bf16, i16 = jnp.float32, jnp.bfloat16, jnp.int16
    return pl.pallas_call(
        whole_kernel,
        name="whole",
        out_shape=(jax.ShapeDtypeStruct((384, PW), f32), jax.ShapeDtypeStruct((384, 768), f32)),
        in_specs=[pl.BlockSpec(memory_space=pltpu.SMEM)] + [VMEM] * 4,
        out_specs=(VMEM, VMEM),
        scratch_shapes=[
            pltpu.VMEM((2, 512, 768), bf16),
            pltpu.VMEM((8, 2, 2, 192, 128), bf16),
            pltpu.VMEM((2, 2, 128, 128), bf16),
            pltpu.VMEM((2, 3, 4, 2, 256, 256), bf16),
            pltpu.VMEM((8, 192, 2048), bf16),
            pltpu.VMEM((128, 2048), bf16),
            pltpu.VMEM((3, 2, 2, 3, 192, 256), i16),
            pltpu.VMEM((3, 2, 2, 3, 8, 256), f32),
            pltpu.VMEM((3, 2, 2, 3, 192, 256), i16),
            pltpu.VMEM((3, 2, 2, 3, 8, 256), f32),
            pltpu.VMEM((2, 3, 2, 192, 256), f32),
            pltpu.VMEM((3, 3, 192, 256), i16),
            pltpu.VMEM((3, 3, 8, 256), f32),
            pltpu.VMEM((3, 3, 192, 256), i16),
            pltpu.VMEM((3, 3, 8, 256), f32),
            pltpu.VMEM((2, 16, 768), f32),
            pltpu.VMEM((2, 4, 2, 16, 768), f32),
            pltpu.VMEM((3, 2, 2, 16, 768), f32),
            pltpu.VMEM((2, 2, 16, 768), f32),
            pltpu.VMEM((3, 16, 768), f32),
            pltpu.VMEM((2, 2, 4, 2, 16, 768), f32),
            pltpu.VMEM((PW, 768), bf16),
            pltpu.VMEM((PW, 768), bf16),
            pltpu.VMEM((PW, PW), f32),
            pltpu.VMEM((384, PW), i16),
            pltpu.VMEM((8, PW), f32),
            sems(1), sems(27), pltpu.SemaphoreType.DMA((9,)), sems(18), sems(18), sems(3), sems(3), sems(3),
            sems(6), sems(6), sems(9), sems(9), sems(9), sems(9),
            sems(32), sems(6), sems(3), sems(7), sems(1), sems(7), sems(7), sems(7),
        ],
        compiler_params=pltpu.CompilerParams(collective_id=0, has_side_effects=True, vmem_limit_bytes=LIMIT),
    )(structure, jnp.swapaxes(lower_panels, 2, 3), upper_panels, given_inverse, ancestor_entries)


def solution(mesh):
    return jax.shard_map(
        local,
        mesh=mesh,
        in_specs=(
            P("depth", None, None, ("rows", "cols")),
            P("depth", "rows", "cols"),
            P("depth", "rows", None),
            P("depth", None),
            P(("depth", "rows"), "cols"),
        ),
        out_specs=(P(("depth", "rows"), None), P(("depth", "rows"), "cols")),
        check_vma=False,
    )
```

```python
import functools

import jax
import jax.numpy as jnp
from jax import lax
from jax.experimental import pallas as pl
from jax.experimental.pallas import tpu as pltpu
from jax.sharding import PartitionSpec as P

PW = 512
MESH = pl.DeviceIdType.MESH
VMEM = pl.BlockSpec(memory_space=pltpu.VMEM)
LIMIT = 58 * 1024 * 1024
OFFSETS = (2, 1, 3, 0)
TOP = 32000.0


def place():
    depth, rows, cols = lax.axis_index("depth"), lax.axis_index("rows"), lax.axis_index("cols")
    return depth // 4, depth % 4, rows, cols // 2, cols % 2


def device(low, z, core, x, half):
    return (low * 4 + z, core, x * 2 + half)


def quantize(value, axis):
    most = jnp.maximum(jnp.max(jnp.abs(value), axis=axis, keepdims=True), 1e-30)
    return jnp.round(value * (TOP / most)).astype(jnp.int16), most / TOP


def split(value):
    high = value.astype(jnp.bfloat16)
    return high, (value - high.astype(jnp.float32)).astype(jnp.bfloat16)


def product(a, b):
    return jnp.dot(a, b, preferred_element_type=jnp.float32)


def dot3(a, b):
    (ah, al), (bh, bl) = split(a), split(b)
    return product(ah, bh) + (product(ah, bl) + product(al, bh))


def received(copies):
    for copy in copies:
        copy.wait_recv()


def whole_kernel(
    kept_ref, low_ref, up_ref, inv_ref, ent_ref, cf_ref, out_ref,
    up_other, turned, turned_top, app, lg, lg_top, cq, cs, rq, rs, own, sq, ss, tq, ts,
    ent_top, ctop, rtop, stop, ttop, top, top_high, top_low, inverse, cf, cf_scale,
    up_sem, l1_sem, loc_sem, l2_sem, f_sem, core_sem, half_sem, fwd_sem,
    r1_sem, r1s_sem, r1b_sem, r1bs_sem, r2_sem, r2s_sem,
    ent_sem, rt_sem, r2t_sem, tg_sem, tc_sem, cf_sem, cfs_sem, cg_sem,
):
    low, z, core, x, half = place()
    depth, col = low * 4 + z, x * 2 + half

    def remote(src, dst, sems, index, target):
        return pltpu.make_async_remote_copy(
            src_ref=src, dst_ref=dst, send_sem=sems.at[0, index], recv_sem=sems.at[1, index],
            device_id=target, device_id_type=MESH,
        )

    partner = device(low, z, 1 - core, x, half)
    across = device(low, z, core, x, 1 - half)
    across_core = device(low, z, 1 - core, x, 1 - half)
    right = device(low, z, core, (x + 1) % 4, half)
    left = device(low, z, core, (x + 3) % 4, half)
    along_z = {o: device(low, (z + o) % 4, core, x, half) for o in (1, 2, 3)}
    along_y = [
        across,
        device(1 - low, z, core, x, half),
        device(1 - low, z, core, x, 1 - half),
    ]

    barrier = pltpu.get_barrier_semaphore()
    friends = [((depth + o // 2) % 8, core if o % 2 == 0 else 1 - core, col) for o in range(1, 16)]
    friends += [(depth, core, (col + o) % 8) for o in range(1, 8)]
    friends += [across_core, along_y[2]]
    for friend in friends:
        pl.semaphore_signal(barrier, inc=1, device_id=friend, device_id_type=MESH)
    upper_copy = remote(up_ref, up_other, up_sem, 0, partner)

    def entry_copy(g, row):
        target = ((g % 2) * 4 + (g // 2) % 4, g // 16, col)
        return pltpu.make_async_remote_copy(
            src_ref=ent_ref.at[pl.ds(pl.multiple_of(row * 16, 16), 16)], dst_ref=ent_top.at[(g // 8) % 2],
            send_sem=ent_sem.at[0, g], recv_sem=ent_sem.at[1, (g // 8) % 2],
            device_id=target, device_id_type=MESH,
        )

    holder = [(depth == 0) & (core == c) for c in range(2)]
    groups = ([g for g in range(24) if g not in (0, 8)], [g for g in range(25, 32)])
    stays = ([(0, 0), (8, 1)], [(24, 1)])

    def entries(act):
        for c in range(2):

            @pl.when(holder[c])
            def _():
                for g in groups[c]:
                    act(entry_copy(g, g - 24 * c))

    def wait_entries():
        @pl.when((depth != 0) | (core != 0))
        def _():
            for h in range(2):

                @pl.when((depth != 0) | (h == 0))
                def _():
                    pltpu.make_async_remote_copy(
                        src_ref=ent_ref.at[pl.ds(0, 16)], dst_ref=ent_top.at[h],
                        send_sem=ent_sem.at[0, 0], recv_sem=ent_sem.at[1, h],
                        device_id=partner, device_id_type=MESH,
                    ).wait_recv()

    def factor(s, block):
        return jnp.full((1, 128), kept_ref[s, block].astype(jnp.float32), jnp.float32)

    lane = pl.multiple_of((x * 4 + core * 2 + half) * 128, 128)
    sharers = ((across, core, 1 - half), (across_core, 1 - core, 1 - half), (partner, 1 - core, half))

    def turn_over(j, part):
        lanes = slice(part * 128, part * 128 + 128)
        both = jnp.concatenate(
            [low_ref[s, j, :, lanes] * factor(s, j * 6 + part).astype(jnp.bfloat16) for s in range(2)]
        )
        return both.T

    def share(src, dst, first):
        here = pltpu.make_async_copy(src(core, half), dst, loc_sem.at[first // 3])
        here.start()
        sends = []
        for t, (target, r, h) in enumerate(sharers):
            copy = remote(src(r, h), dst, l1_sem, first + t, target)
            copy.start()
            sends.append(copy)
        return here, sends

    def turn_top():
        for part in range(4):
            turned_top[part // 2, part % 2] = turn_over(0, part)

    def share_top():
        return share(lambda r, h: turned_top.at[r, h], lg_top.at[:, pl.ds(lane, 128)], 24)

    def turn_rows(q):
        j = (q % 2) * 4 + (z + OFFSETS[q // 2]) % 4
        for part in range(6):
            value = turn_over(j, part)
            for piece in range(2):
                row = part * 128 + piece * 64
                turned[q, row // 384, (row // 192) % 2, row % 192:row % 192 + 64] = (
                    value[piece * 64:piece * 64 + 64]
                )

    def share_rows(q):
        return share(lambda r, h: turned.at[q, r, h], lg.at[q, :, pl.ds(lane, 128)], q * 3)

    mine, theirs = pl.multiple_of(core * 512, 512), pl.multiple_of((1 - core) * 512, 512)

    def apply(tile):
        cols = slice(tile * 256, tile * 256 + 256)
        for s in range(2):
            total = product(inv_ref[s, :, pl.ds(mine, 512)], up_ref[s, :, cols]) + product(
                inv_ref[s, :, pl.ds(theirs, 512)], up_other[s, :, cols]
            )
            block = col * 6 + tile * 2
            mask = jnp.concatenate([factor(s, block), factor(s, block + 1)], axis=1)
            applied = (total * mask).astype(jnp.bfloat16)
            for c in range(8):
                app[half, tile, c // 2, core, (c % 2) * 128 + s * 64:(c % 2) * 128 + s * 64 + 64] = (
                    applied[c * 64:(c + 1) * 64]
                )
        part = app.at[half, tile, :, core]
        copies = [remote(part, part, core_sem, tile, partner), remote(part, part, half_sem, tile, across)]
        copies[0].start()
        return copies

    def forward_applied(tile):
        part = app.at[1 - half, tile, :, core]
        copy = remote(part, part, fwd_sem, tile, partner)
        copy.start()
        return copy

    at_home = pl.ds(pl.multiple_of(x * 512, 512), 512)
    from_left = pl.ds(pl.multiple_of(((x + 3) % 4) * 512, 512), 512)
    from_right = pl.ds(pl.multiple_of(((x + 1) % 4) * 512, 512), 512)

    def both_ways(first, second, sems, q):
        copies = [remote(first, first, sems, q * 2, right), remote(second, second, sems, q * 2 + 1, left)]
        for copy in copies:
            copy.start()
        return copies

    def rows_of(q):
        return (lg_top, 64) if q == 8 else (lg.at[q], 96)

    def ring(q):
        block = rows_of(q)[0].at[:, at_home]
        return both_ways(block, block, l2_sem, q)

    def forward(q):
        rows, count = rows_of(q)
        return both_ways(
            rows.at[pl.ds(0, count), from_left], rows.at[pl.ds(count, count), from_right], f_sem, q
        )

    sides = (half, 1 - half)

    def own_copies(q):
        o, b = OFFSETS[q // 2], q % 2
        return (
            remote(cq.at[o - 1, b, 0], rq.at[o - 1, b, 0], r1_sem, q, along_z[o]),
            remote(cs.at[o - 1, b, 0], rs.at[o - 1, b, 0], r1s_sem, q, along_z[o]),
        )

    def give_own(q):
        o, b = OFFSETS[q // 2], q % 2

        @pl.loop(0, 3)
        def _(tile):
            total = product(lg[q], app[half, tile].reshape(2048, 256))
            if o == 0:
                own[0, tile, b] = total
            else:
                values, scale = quantize(total, 0)
                cq[o - 1, b, 0, tile] = values
                cs[o - 1, b, 0, tile] = jnp.broadcast_to(scale, (8, 256))

        if o != 0:
            for copy in own_copies(q):
                copy.start()

    def other_copies(g, tile):
        o = OFFSETS[g]
        return (
            remote(cq.at[o - 1, :, 1, tile], rq.at[o - 1, :, 1, tile], r1b_sem, g * 3 + tile, along_z[o]),
            remote(cs.at[o - 1, :, 1, tile], rs.at[o - 1, :, 1, tile], r1bs_sem, g * 3 + tile, along_z[o]),
        )

    def give_other(g, tile):
        o = OFFSETS[g]
        total = product(
            lg[g * 2:g * 2 + 2].reshape(384, 2048), app[1 - half, tile].reshape(2048, 256)
        ).reshape(2, 192, 256)
        if o == 0:
            own[1, tile] = total
            return
        values, scale = quantize(total, 1)
        for b in range(2):
            cq[o - 1, b, 1, tile] = values[b]
            cs[o - 1, b, 1, tile] = jnp.broadcast_to(scale[b], (8, 256))
        for copy in other_copies(g, tile):
            copy.start()

    def make_top(turn, tile):
        total = product(lg_top[...], app[sides[turn], tile].reshape(2048, 256))
        ctop[turn, :, :, :, tile * 256:tile * 256 + 256] = total.reshape(4, 2, 16, 256)

    def top_copies(turn):
        return [
            remote(ctop.at[turn, (z + o) % 4], rtop.at[o - 1, turn], rt_sem, turn * 3 + o - 1, along_z[o])
            for o in (1, 2, 3)
        ]

    def give_top(turn):
        copies = top_copies(turn)
        for copy in copies:
            copy.start()
        return copies

    def sum_top():
        received(tops[0])
        received(tops[1])
        for turn in range(2):
            total = ctop[turn, z]
            for o in range(3):
                total = total + rtop[o, turn]
            stop[turn] = total
        top_moves = [
            remote(stop.at[turn, row], ttop.at[t], r2t_sem, t, along_y[t])
            for t, (turn, row) in enumerate(((1, low), (0, 1 - low), (1, 1 - low)))
        ]
        for copy in top_moves:
            copy.start()
        return top_moves

    def gather_top():
        received(top_moves)
        wait_entries()

        top[core, half, z, low] = ent_top[half] - (stop[0, low] + ttop[1])
        top[core, 1 - half, z, low] = ent_top[1 - half] - (ttop[0] + ttop[2])
        gathers = []
        for o in range(1, 8):
            piece = top.at[core, :, z, low]
            copy = remote(piece, piece, tg_sem, o - 1, ((depth + o) % 8, core, col))
            copy.start()
            gathers.append(copy)
        return gathers

    stage1, stage2, passed, applied, onward, tops = {}, {}, {}, {}, {}, {}

    def start_ring(q):
        stage1[q][0].wait()
        received(stage1[q][1])
        stage2[q] = ring(q)

    turn_top()
    turn_rows(0)
    pl.semaphore_wait(barrier, len(friends))
    stage1[8] = share_top()
    stage1[0] = share_rows(0)
    upper_copy.start()
    for q in range(1, 4):
        turn_rows(q)
        stage1[q] = share_rows(q)
    start_ring(8)
    start_ring(0)
    entries(lambda copy: copy.start())
    for c in range(2):

        @pl.when(holder[c])
        def _():
            for g, h in stays[c]:
                row = (g - 24 * c) * 16
                ent_top[h] = ent_ref[row:row + 16, :]

    upper_copy.wait()
    applied[0] = apply(0)
    start_ring(1)
    for q in range(4, 6):
        turn_rows(q)
        stage1[q] = share_rows(q)
    applied[0][1].start()
    for q in range(6, 8):
        turn_rows(q)
        stage1[q] = share_rows(q)
    received(stage2[8])
    passed[8] = forward(8)
    applied[1] = apply(1)
    applied[1][1].start()
    applied[2] = apply(2)
    applied[2][1].start()

    for q in range(8):
        received(stage2[q])
        passed[q] = forward(q)
        if q + 2 < 8:
            start_ring(q + 2)
        if q == 0:
            received([applied[t][0] for t in range(3)])
            received(passed[8])
            for tile in range(3):
                make_top(0, tile)
            tops[0] = give_top(0)
        else:
            received(passed[q - 1])
            give_own(q - 1)
        if q in (1, 3, 5):
            tile = q // 2
            applied[tile][1].wait_recv()
            onward[tile] = forward_applied(tile)
        if q in (2, 4, 6):
            onward[q // 2 - 1].wait_recv()
            make_top(1, q // 2 - 1)
        if q == 2:
            give_other(0, 0)
        if q == 4:
            give_other(1, 0)
            give_other(0, 1)
        if q == 5:
            give_other(1, 1)
        if q == 6:
            tops[1] = give_top(1)
            give_other(2, 0)
        if q == 7:
            top_moves = sum_top()
            give_other(0, 2)
            give_other(1, 2)
            gathers = gather_top()
            give_other(2, 1)
            give_other(2, 2)
    received(passed[7])
    give_own(7)
    for tile in range(3):
        give_other(3, tile)

    def chunk_sum(turn, row, tile):
        total = own[turn, tile, row]
        for o in range(3):
            total = total + rq[o, row, turn, tile].astype(jnp.float32) * rs[o, row, turn, tile, 0:1, :]
        return total

    moved = []

    def hand(t, turn, row, tile):
        values, scale = quantize(chunk_sum(turn, row, tile), 0)
        sq[t, tile] = values
        ss[t, tile] = jnp.broadcast_to(scale, (8, 256))
        copies = [
            remote(sq.at[t, tile], tq.at[t, tile], r2_sem, t * 3 + tile, along_y[t]),
            remote(ss.at[t, tile], ts.at[t, tile], r2s_sem, t * 3 + tile, along_y[t]),
        ]
        for copy in copies:
            copy.start()
        moved.extend(copies)

    for q in range(6):
        received(own_copies(q))
    for tile in range(3):
        hand(1, 0, 1 - low, tile)

    for tile in range(3):
        for g in range(3):
            received(other_copies(g, tile))
        hand(0, 1, low, tile)
        hand(2, 1, 1 - low, tile)
    received(gathers)
    core_copy = remote(top.at[core], top.at[core], tc_sem, 0, partner)
    core_copy.start()

    def arrived(t, tile):
        return tq[t, tile].astype(jnp.float32) * ts[t, tile, 0:1, :]

    mine = pl.ds(pl.multiple_of(half * 192, 192), 192)
    other = pl.ds(pl.multiple_of((1 - half) * 192, 192), 192)
    received(moved[0:6])
    for tile in range(3):
        cols = slice(tile * 256, tile * 256 + 256)
        out_ref[mine, cols] = ent_ref[mine, cols] - (chunk_sum(0, low, tile) + arrived(1, tile))
    for tile in range(3):
        received(moved[6 + tile * 4:10 + tile * 4])
        cols = slice(tile * 256, tile * 256 + 256)
        out_ref[other, cols] = ent_ref[other, cols] - (arrived(0, tile) + arrived(2, tile))

    core_copy.wait_recv()

    @pl.when(col == 0)
    def _():
        row = lax.broadcasted_iota(jnp.int32, (PW, PW), 0)
        identity = (row == lax.broadcasted_iota(jnp.int32, (PW, PW), 1)).astype(jnp.float32)
        pivot = top[:, :, :, :, :, :PW].reshape(PW, PW)
        error = identity - pivot * (1.0 / 16.0)
        square = dot3(error, error)
        inverse[...] = dot3(identity + error, identity + square) * (1.0 / 16.0)

    bounds = (0, 64, 128, 192, 240, 288, 336, 384)

    def piece(c):
        return cf.at[bounds[c - 1]:bounds[c]]

    def scale_copy(c):
        return remote(cf_scale, cf_scale, cfs_sem, c - 1, (depth, core, c))

    first_row = depth * 768 + core * 384
    unit = (
        lax.broadcasted_iota(jnp.int32, (384, PW), 0) + first_row == lax.broadcasted_iota(jnp.int32, (384, PW), 1)
    ).astype(jnp.float32)

    def cf_copy(c):
        return remote(piece(c), piece(c), cf_sem, c - 1, (depth, core, c))

    def hand_on(c, target):
        return pltpu.make_async_remote_copy(
            src_ref=piece(c), dst_ref=piece(c), send_sem=cg_sem.at[0, target - 1], recv_sem=cg_sem.at[1, c - 1],
            device_id=(depth, core, target), device_id_type=MESH,
        )

    @pl.when(col == 0)
    def _():
        values, scale = quantize(dot3(out_ref[:, :PW], inverse[...]) - unit, 0)
        cf[...] = values
        cf_scale[...] = jnp.broadcast_to(scale, (8, PW))
        for c in (4, 5, 2, 3, 6, 7, 1):
            cf_copy(c).start()
        for c in range(1, 8):
            scale_copy(c).start()

    for tile in range(3):
        cols = slice(tile * 256, tile * 256 + 256)
        high, rest = split(top[:, :, :, :, :, cols].reshape(PW, 256))
        top_high[:, cols] = high
        top_low[:, cols] = rest

    @pl.when(col == 0)
    def _():
        for c in range(1, 8):
            cf_copy(c).wait_send()
            scale_copy(c).wait_send()

    for c in range(1, 8):

        @pl.when(col == c)
        def _():
            cf_copy(c).wait_recv()
            others = [k for k in range(1, 8) if k != c]
            copies = [hand_on(c, k) for k in others]
            for copy in copies:
                copy.start()
            for k in others:
                hand_on(k, k).wait_recv()
            scale_copy(c).wait_recv()
            for copy in copies:
                copy.wait_send()

    column = cf[...].astype(jnp.float32) * cf_scale[0:1, :] + unit
    cf_ref[...] = column
    column_high, column_low = split(column)
    for tile in range(3):
        cols = slice(tile * 256, tile * 256 + 256)
        th, tl = top_high[:, cols], top_low[:, cols]
        out_ref[:, cols] = out_ref[:, cols] - (
            product(column_high, th) + (product(column_high, tl) + product(column_low, th))
        )

    for group in (
        *(sends for _, sends in stage1.values()), *stage2.values(), *passed.values(), *applied.values(),
        onward.values(), tops[0], tops[1], top_moves, gathers, [core_copy], moved,
    ):
        for copy in group:
            copy.wait_send()
    for q in range(6):
        for copy in own_copies(q):
            copy.wait_send()
    for g in range(3):
        for tile in range(3):
            for copy in other_copies(g, tile):
                copy.wait_send()
    entries(lambda copy: copy.wait_send())


def sems(count):
    return pltpu.SemaphoreType.DMA((2, count))


def local(lower_panels, upper_panels, given_inverse, structure, ancestor_entries):
    f32, bf16, i16 = jnp.float32, jnp.bfloat16, jnp.int16
    return pl.pallas_call(
        whole_kernel,
        name="whole",
        out_shape=(jax.ShapeDtypeStruct((384, PW), f32), jax.ShapeDtypeStruct((384, 768), f32)),
        in_specs=[pl.BlockSpec(memory_space=pltpu.SMEM)] + [VMEM] * 4,
        out_specs=(VMEM, VMEM),
        scratch_shapes=[
            pltpu.VMEM((2, 512, 768), bf16),
            pltpu.VMEM((8, 2, 2, 192, 128), bf16),
            pltpu.VMEM((2, 2, 128, 128), bf16),
            pltpu.VMEM((2, 3, 4, 2, 256, 256), bf16),
            pltpu.VMEM((8, 192, 2048), bf16),
            pltpu.VMEM((128, 2048), bf16),
            pltpu.VMEM((3, 2, 2, 3, 192, 256), i16),
            pltpu.VMEM((3, 2, 2, 3, 8, 256), f32),
            pltpu.VMEM((3, 2, 2, 3, 192, 256), i16),
            pltpu.VMEM((3, 2, 2, 3, 8, 256), f32),
            pltpu.VMEM((2, 3, 2, 192, 256), f32),
            pltpu.VMEM((3, 3, 192, 256), i16),
            pltpu.VMEM((3, 3, 8, 256), f32),
            pltpu.VMEM((3, 3, 192, 256), i16),
            pltpu.VMEM((3, 3, 8, 256), f32),
            pltpu.VMEM((2, 16, 768), f32),
            pltpu.VMEM((2, 4, 2, 16, 768), f32),
            pltpu.VMEM((3, 2, 2, 16, 768), f32),
            pltpu.VMEM((2, 2, 16, 768), f32),
            pltpu.VMEM((3, 16, 768), f32),
            pltpu.VMEM((2, 2, 4, 2, 16, 768), f32),
            pltpu.VMEM((PW, 768), bf16),
            pltpu.VMEM((PW, 768), bf16),
            pltpu.VMEM((PW, PW), f32),
            pltpu.VMEM((384, PW), i16),
            pltpu.VMEM((8, PW), f32),
            sems(1), sems(27), pltpu.SemaphoreType.DMA((9,)), sems(18), sems(18), sems(3), sems(3), sems(3),
            sems(6), sems(6), sems(9), sems(9), sems(9), sems(9),
            sems(32), sems(6), sems(3), sems(7), sems(1), sems(7), sems(7), sems(7),
        ],
        compiler_params=pltpu.CompilerParams(collective_id=0, has_side_effects=True, vmem_limit_bytes=LIMIT),
    )(structure, jnp.swapaxes(lower_panels, 2, 3), upper_panels, given_inverse, ancestor_entries)


def solution(mesh):
    return jax.shard_map(
        local,
        mesh=mesh,
        in_specs=(
            P("depth", None, None, ("rows", "cols")),
            P("depth", "rows", "cols"),
            P("depth", "rows", None),
            P("depth", None),
            P(("depth", "rows"), "cols"),
        ),
        out_specs=(P(("depth", "rows"), None), P(("depth", "rows"), "cols")),
        check_vma=False,
    )
```

```python
import functools

import jax
import jax.numpy as jnp
from jax import lax
from jax.experimental import pallas as pl
from jax.experimental.pallas import tpu as pltpu
from jax.sharding import PartitionSpec as P

PW = 512
MESH = pl.DeviceIdType.MESH
VMEM = pl.BlockSpec(memory_space=pltpu.VMEM)
LIMIT = 58 * 1024 * 1024
OFFSETS = (2, 1, 3, 0)
TOP = 32000.0


def place():
    depth, rows, cols = lax.axis_index("depth"), lax.axis_index("rows"), lax.axis_index("cols")
    return depth // 4, depth % 4, rows, cols // 2, cols % 2


def device(low, z, core, x, half):
    return (low * 4 + z, core, x * 2 + half)


def quantize(value, axis):
    most = jnp.maximum(jnp.max(jnp.abs(value), axis=axis, keepdims=True), 1e-30)
    return jnp.round(value * (TOP / most)).astype(jnp.int16), most / TOP


def split(value):
    high = value.astype(jnp.bfloat16)
    return high, (value - high.astype(jnp.float32)).astype(jnp.bfloat16)


def product(a, b):
    return jnp.dot(a, b, preferred_element_type=jnp.float32)


def dot3(a, b):
    (ah, al), (bh, bl) = split(a), split(b)
    return product(ah, bh) + (product(ah, bl) + product(al, bh))


def received(copies):
    for copy in copies:
        copy.wait_recv()


def whole_kernel(
    kept_ref, low_ref, up_ref, inv_ref, ent_ref, cf_ref, out_ref,
    up_other, turned, turned_top, app, lg, lg_top, cq, cs, rq, rs, own, sq, ss, tq, ts,
    ent_top, ctop, rtop, stop, ttop, top, top_high, top_low, inverse, cf, cf_scale,
    up_sem, l1_sem, loc_sem, l2_sem, f_sem, core_sem, half_sem, fwd_sem,
    r1_sem, r1s_sem, r1b_sem, r1bs_sem, r2_sem, r2s_sem,
    ent_sem, rt_sem, r2t_sem, tg_sem, tc_sem, cf_sem, cfs_sem, cg_sem,
):
    low, z, core, x, half = place()
    depth, col = low * 4 + z, x * 2 + half

    def remote(src, dst, sems, index, target):
        return pltpu.make_async_remote_copy(
            src_ref=src, dst_ref=dst, send_sem=sems.at[0, index], recv_sem=sems.at[1, index],
            device_id=target, device_id_type=MESH,
        )

    partner = device(low, z, 1 - core, x, half)
    across = device(low, z, core, x, 1 - half)
    across_core = device(low, z, 1 - core, x, 1 - half)
    right = device(low, z, core, (x + 1) % 4, half)
    left = device(low, z, core, (x + 3) % 4, half)
    along_z = {o: device(low, (z + o) % 4, core, x, half) for o in (1, 2, 3)}
    along_y = [
        across,
        device(1 - low, z, core, x, half),
        device(1 - low, z, core, x, 1 - half),
    ]

    barrier = pltpu.get_barrier_semaphore()
    friends = [((depth + o // 2) % 8, core if o % 2 == 0 else 1 - core, col) for o in range(1, 16)]
    friends += [(depth, core, (col + o) % 8) for o in range(1, 8)]
    friends += [across_core, along_y[2]]
    for friend in friends:
        pl.semaphore_signal(barrier, inc=1, device_id=friend, device_id_type=MESH)
    upper_copy = remote(up_ref, up_other, up_sem, 0, partner)

    def entry_copy(g, row):
        target = ((g % 2) * 4 + (g // 2) % 4, g // 16, col)
        return pltpu.make_async_remote_copy(
            src_ref=ent_ref.at[pl.ds(pl.multiple_of(row * 16, 16), 16)], dst_ref=ent_top.at[(g // 8) % 2],
            send_sem=ent_sem.at[0, g], recv_sem=ent_sem.at[1, (g // 8) % 2],
            device_id=target, device_id_type=MESH,
        )

    holder = [(depth == 0) & (core == c) for c in range(2)]
    groups = ([g for g in range(24) if g not in (0, 8)], [g for g in range(25, 32)])
    stays = ([(0, 0), (8, 1)], [(24, 1)])

    def entries(act):
        for c in range(2):

            @pl.when(holder[c])
            def _():
                for g in groups[c]:
                    act(entry_copy(g, g - 24 * c))

    def wait_entries():
        @pl.when((depth != 0) | (core != 0))
        def _():
            for h in range(2):

                @pl.when((depth != 0) | (h == 0))
                def _():
                    pltpu.make_async_remote_copy(
                        src_ref=ent_ref.at[pl.ds(0, 16)], dst_ref=ent_top.at[h],
                        send_sem=ent_sem.at[0, 0], recv_sem=ent_sem.at[1, h],
                        device_id=partner, device_id_type=MESH,
                    ).wait_recv()

    def factor(s, block):
        return jnp.full((1, 128), kept_ref[s, block].astype(jnp.float32), jnp.float32)

    lane = pl.multiple_of((x * 4 + core * 2 + half) * 128, 128)
    sharers = ((across, core, 1 - half), (across_core, 1 - core, 1 - half), (partner, 1 - core, half))

    def turn_over(j, part):
        lanes = slice(part * 128, part * 128 + 128)
        both = jnp.concatenate(
            [low_ref[s, j, :, lanes] * factor(s, j * 6 + part).astype(jnp.bfloat16) for s in range(2)]
        )
        return both.T

    def share(src, dst, first):
        here = pltpu.make_async_copy(src(core, half), dst, loc_sem.at[first // 3])
        here.start()
        sends = []
        for t, (target, r, h) in enumerate(sharers):
            copy = remote(src(r, h), dst, l1_sem, first + t, target)
            copy.start()
            sends.append(copy)
        return here, sends

    def turn_top():
        for part in range(4):
            turned_top[part // 2, part % 2] = turn_over(0, part)

    def share_top():
        return share(lambda r, h: turned_top.at[r, h], lg_top.at[:, pl.ds(lane, 128)], 24)

    def turn_rows(q):
        j = (q % 2) * 4 + (z + OFFSETS[q // 2]) % 4
        for part in range(6):
            value = turn_over(j, part)
            for piece in range(2):
                row = part * 128 + piece * 64
                turned[q, row // 384, (row // 192) % 2, row % 192:row % 192 + 64] = (
                    value[piece * 64:piece * 64 + 64]
                )

    def share_rows(q):
        return share(lambda r, h: turned.at[q, r, h], lg.at[q, :, pl.ds(lane, 128)], q * 3)

    mine, theirs = pl.multiple_of(core * 512, 512), pl.multiple_of((1 - core) * 512, 512)

    def apply(tile):
        cols = slice(tile * 256, tile * 256 + 256)
        for s in range(2):
            total = product(inv_ref[s, :, pl.ds(mine, 512)], up_ref[s, :, cols]) + product(
                inv_ref[s, :, pl.ds(theirs, 512)], up_other[s, :, cols]
            )
            block = col * 6 + tile * 2
            mask = jnp.concatenate([factor(s, block), factor(s, block + 1)], axis=1)
            applied = (total * mask).astype(jnp.bfloat16)
            for c in range(8):
                app[half, tile, c // 2, core, (c % 2) * 128 + s * 64:(c % 2) * 128 + s * 64 + 64] = (
                    applied[c * 64:(c + 1) * 64]
                )
        part = app.at[half, tile, :, core]
        copies = [remote(part, part, core_sem, tile, partner), remote(part, part, half_sem, tile, across)]
        copies[0].start()
        return copies

    def forward_applied(tile):
        part = app.at[1 - half, tile, :, core]
        copy = remote(part, part, fwd_sem, tile, partner)
        copy.start()
        return copy

    at_home = pl.ds(pl.multiple_of(x * 512, 512), 512)
    from_left = pl.ds(pl.multiple_of(((x + 3) % 4) * 512, 512), 512)
    from_right = pl.ds(pl.multiple_of(((x + 1) % 4) * 512, 512), 512)

    def both_ways(first, second, sems, q):
        copies = [remote(first, first, sems, q * 2, right), remote(second, second, sems, q * 2 + 1, left)]
        for copy in copies:
            copy.start()
        return copies

    def rows_of(q):
        return (lg_top, 64) if q == 8 else (lg.at[q], 96)

    def ring(q):
        block = rows_of(q)[0].at[:, at_home]
        return both_ways(block, block, l2_sem, q)

    def forward(q):
        rows, count = rows_of(q)
        return both_ways(
            rows.at[pl.ds(0, count), from_left], rows.at[pl.ds(count, count), from_right], f_sem, q
        )

    sides = (half, 1 - half)

    def own_copies(q):
        o, b = OFFSETS[q // 2], q % 2
        return (
            remote(cq.at[o - 1, b, 0], rq.at[o - 1, b, 0], r1_sem, q, along_z[o]),
            remote(cs.at[o - 1, b, 0], rs.at[o - 1, b, 0], r1s_sem, q, along_z[o]),
        )

    def give_own(q):
        o, b = OFFSETS[q // 2], q % 2

        @pl.loop(0, 3)
        def _(tile):
            total = product(lg[q], app[half, tile].reshape(2048, 256))
            if o == 0:
                own[0, tile, b] = total
            else:
                values, scale = quantize(total, 0)
                cq[o - 1, b, 0, tile] = values
                cs[o - 1, b, 0, tile] = jnp.broadcast_to(scale, (8, 256))

        if o != 0:
            for copy in own_copies(q):
                copy.start()

    def other_copies(g, tile):
        o = OFFSETS[g]
        return (
            remote(cq.at[o - 1, :, 1, tile], rq.at[o - 1, :, 1, tile], r1b_sem, g * 3 + tile, along_z[o]),
            remote(cs.at[o - 1, :, 1, tile], rs.at[o - 1, :, 1, tile], r1bs_sem, g * 3 + tile, along_z[o]),
        )

    def give_other(g, tile):
        o = OFFSETS[g]
        total = product(
            lg[g * 2:g * 2 + 2].reshape(384, 2048), app[1 - half, tile].reshape(2048, 256)
        ).reshape(2, 192, 256)
        if o == 0:
            own[1, tile] = total
            return
        values, scale = quantize(total, 1)
        for b in range(2):
            cq[o - 1, b, 1, tile] = values[b]
            cs[o - 1, b, 1, tile] = jnp.broadcast_to(scale[b], (8, 256))
        for copy in other_copies(g, tile):
            copy.start()

    def make_top(turn, tile):
        total = product(lg_top[...], app[sides[turn], tile].reshape(2048, 256))
        ctop[turn, :, :, :, tile * 256:tile * 256 + 256] = total.reshape(4, 2, 16, 256)

    def top_copies(turn):
        return [
            remote(ctop.at[turn, (z + o) % 4], rtop.at[o - 1, turn], rt_sem, turn * 3 + o - 1, along_z[o])
            for o in (1, 2, 3)
        ]

    def give_top(turn):
        copies = top_copies(turn)
        for copy in copies:
            copy.start()
        return copies

    def sum_top():
        received(tops[0])
        received(tops[1])
        for turn in range(2):
            total = ctop[turn, z]
            for o in range(3):
                total = total + rtop[o, turn]
            stop[turn] = total
        top_moves = [
            remote(stop.at[turn, row], ttop.at[t], r2t_sem, t, along_y[t])
            for t, (turn, row) in enumerate(((1, low), (0, 1 - low), (1, 1 - low)))
        ]
        for copy in top_moves:
            copy.start()
        return top_moves

    def gather_top():
        received(top_moves)
        wait_entries()

        top[core, half, z, low] = ent_top[half] - (stop[0, low] + ttop[1])
        top[core, 1 - half, z, low] = ent_top[1 - half] - (ttop[0] + ttop[2])
        gathers = []
        for o in range(1, 8):
            piece = top.at[core, :, z, low]
            copy = remote(piece, piece, tg_sem, o - 1, ((depth + o) % 8, core, col))
            copy.start()
            gathers.append(copy)
        return gathers

    stage1, stage2, passed, applied, onward, tops = {}, {}, {}, {}, {}, {}

    def start_ring(q):
        stage1[q][0].wait()
        received(stage1[q][1])
        stage2[q] = ring(q)

    turn_top()
    turn_rows(0)
    pl.semaphore_wait(barrier, len(friends))
    stage1[8] = share_top()
    stage1[0] = share_rows(0)
    upper_copy.start()
    for q in range(1, 4):
        turn_rows(q)
        stage1[q] = share_rows(q)
    start_ring(8)
    start_ring(0)
    entries(lambda copy: copy.start())
    for c in range(2):

        @pl.when(holder[c])
        def _():
            for g, h in stays[c]:
                row = (g - 24 * c) * 16
                ent_top[h] = ent_ref[row:row + 16, :]

    upper_copy.wait()
    applied[0] = apply(0)
    start_ring(1)
    for q in range(4, 6):
        turn_rows(q)
        stage1[q] = share_rows(q)
    applied[0][1].start()
    for q in range(6, 8):
        turn_rows(q)
        stage1[q] = share_rows(q)
    received(stage2[8])
    passed[8] = forward(8)
    applied[1] = apply(1)
    applied[1][1].start()
    applied[2] = apply(2)
    applied[2][1].start()

    for q in range(8):
        received(stage2[q])
        passed[q] = forward(q)
        if q + 2 < 8:
            start_ring(q + 2)
        if q == 0:
            received([applied[t][0] for t in range(3)])
            received(passed[8])
            for tile in range(3):
                make_top(0, tile)
            tops[0] = give_top(0)
        else:
            received(passed[q - 1])
            give_own(q - 1)
        if q in (1, 3, 5):
            tile = q // 2
            applied[tile][1].wait_recv()
            onward[tile] = forward_applied(tile)
        if q in (2, 4, 6):
            onward[q // 2 - 1].wait_recv()
            make_top(1, q // 2 - 1)
        if q == 2:
            give_other(0, 0)
        if q == 4:
            give_other(1, 0)
            give_other(0, 1)
        if q == 5:
            give_other(1, 1)
        if q == 6:
            tops[1] = give_top(1)
            give_other(2, 0)
        if q == 7:
            top_moves = sum_top()
            give_other(0, 2)
            give_other(1, 2)
            gathers = gather_top()
            give_other(2, 1)
            give_other(2, 2)
    received(passed[7])
    give_own(7)
    for tile in range(3):
        give_other(3, tile)

    def chunk_sum(turn, row, tile):
        total = own[turn, tile, row]
        for o in range(3):
            total = total + rq[o, row, turn, tile].astype(jnp.float32) * rs[o, row, turn, tile, 0:1, :]
        return total

    moved = []

    def hand(t, turn, row, tile):
        values, scale = quantize(chunk_sum(turn, row, tile), 0)
        sq[t, tile] = values
        ss[t, tile] = jnp.broadcast_to(scale, (8, 256))
        copies = [
            remote(sq.at[t, tile], tq.at[t, tile], r2_sem, t * 3 + tile, along_y[t]),
            remote(ss.at[t, tile], ts.at[t, tile], r2s_sem, t * 3 + tile, along_y[t]),
        ]
        for copy in copies:
            copy.start()
        moved.extend(copies)

    for q in range(6):
        received(own_copies(q))
    for tile in range(3):
        hand(1, 0, 1 - low, tile)

    for tile in range(3):
        for g in range(3):
            received(other_copies(g, tile))
        hand(0, 1, low, tile)
        hand(2, 1, 1 - low, tile)
        if tile == 1:
            received(gathers)
            core_copy = remote(top.at[core], top.at[core], tc_sem, 0, partner)
            core_copy.start()

    def arrived(t, tile):
        return tq[t, tile].astype(jnp.float32) * ts[t, tile, 0:1, :]

    mine = pl.ds(pl.multiple_of(half * 192, 192), 192)
    other = pl.ds(pl.multiple_of((1 - half) * 192, 192), 192)
    received(moved[0:6])
    for tile in range(3):
        cols = slice(tile * 256, tile * 256 + 256)
        out_ref[mine, cols] = ent_ref[mine, cols] - (chunk_sum(0, low, tile) + arrived(1, tile))
    for tile in range(3):
        received(moved[6 + tile * 4:10 + tile * 4])
        cols = slice(tile * 256, tile * 256 + 256)
        out_ref[other, cols] = ent_ref[other, cols] - (arrived(0, tile) + arrived(2, tile))

    core_copy.wait_recv()

    @pl.when(col == 0)
    def _():
        row = lax.broadcasted_iota(jnp.int32, (PW, PW), 0)
        identity = (row == lax.broadcasted_iota(jnp.int32, (PW, PW), 1)).astype(jnp.float32)
        pivot = top[:, :, :, :, :, :PW].reshape(PW, PW)
        error = identity - pivot * (1.0 / 16.0)
        square = dot3(error, error)
        inverse[...] = dot3(identity + error, identity + square) * (1.0 / 16.0)

    bounds = (0, 64, 128, 192, 240, 288, 336, 384)

    def piece(c):
        return cf.at[bounds[c - 1]:bounds[c]]

    def scale_copy(c):
        return remote(cf_scale, cf_scale, cfs_sem, c - 1, (depth, core, c))

    first_row = depth * 768 + core * 384
    unit = (
        lax.broadcasted_iota(jnp.int32, (384, PW), 0) + first_row == lax.broadcasted_iota(jnp.int32, (384, PW), 1)
    ).astype(jnp.float32)

    def cf_copy(c):
        return remote(piece(c), piece(c), cf_sem, c - 1, (depth, core, c))

    def hand_on(c, target):
        return pltpu.make_async_remote_copy(
            src_ref=piece(c), dst_ref=piece(c), send_sem=cg_sem.at[0, target - 1], recv_sem=cg_sem.at[1, c - 1],
            device_id=(depth, core, target), device_id_type=MESH,
        )

    @pl.when(col == 0)
    def _():
        values, scale = quantize(dot3(out_ref[:, :PW], inverse[...]) - unit, 0)
        cf[...] = values
        cf_scale[...] = jnp.broadcast_to(scale, (8, PW))
        for c in (4, 5, 2, 3, 6, 7, 1):
            cf_copy(c).start()
        for c in range(1, 8):
            scale_copy(c).start()

    for tile in range(3):
        cols = slice(tile * 256, tile * 256 + 256)
        high, rest = split(top[:, :, :, :, :, cols].reshape(PW, 256))
        top_high[:, cols] = high
        top_low[:, cols] = rest

    @pl.when(col == 0)
    def _():
        for c in range(1, 8):
            cf_copy(c).wait_send()
            scale_copy(c).wait_send()

    for c in range(1, 8):

        @pl.when(col == c)
        def _():
            cf_copy(c).wait_recv()
            others = [k for k in range(1, 8) if k != c]
            copies = [hand_on(c, k) for k in others]
            for copy in copies:
                copy.start()
            for k in others:
                hand_on(k, k).wait_recv()
            scale_copy(c).wait_recv()
            for copy in copies:
                copy.wait_send()

    column = cf[...].astype(jnp.float32) * cf_scale[0:1, :] + unit
    cf_ref[...] = column
    column_high, column_low = split(column)
    for tile in range(3):
        cols = slice(tile * 256, tile * 256 + 256)
        th, tl = top_high[:, cols], top_low[:, cols]
        out_ref[:, cols] = out_ref[:, cols] - (
            product(column_high, th) + (product(column_high, tl) + product(column_low, th))
        )

    for group in (
        *(sends for _, sends in stage1.values()), *stage2.values(), *passed.values(), *applied.values(),
        onward.values(), tops[0], tops[1], top_moves, gathers, [core_copy], moved,
    ):
        for copy in group:
            copy.wait_send()
    for q in range(6):
        for copy in own_copies(q):
            copy.wait_send()
    for g in range(3):
        for tile in range(3):
            for copy in other_copies(g, tile):
                copy.wait_send()
    entries(lambda copy: copy.wait_send())


def sems(count):
    return pltpu.SemaphoreType.DMA((2, count))


def local(lower_panels, upper_panels, given_inverse, structure, ancestor_entries):
    f32, bf16, i16 = jnp.float32, jnp.bfloat16, jnp.int16
    return pl.pallas_call(
        whole_kernel,
        name="whole",
        out_shape=(jax.ShapeDtypeStruct((384, PW), f32), jax.ShapeDtypeStruct((384, 768), f32)),
        in_specs=[pl.BlockSpec(memory_space=pltpu.SMEM)] + [VMEM] * 4,
        out_specs=(VMEM, VMEM),
        scratch_shapes=[
            pltpu.VMEM((2, 512, 768), bf16),
            pltpu.VMEM((8, 2, 2, 192, 128), bf16),
            pltpu.VMEM((2, 2, 128, 128), bf16),
            pltpu.VMEM((2, 3, 4, 2, 256, 256), bf16),
            pltpu.VMEM((8, 192, 2048), bf16),
            pltpu.VMEM((128, 2048), bf16),
            pltpu.VMEM((3, 2, 2, 3, 192, 256), i16),
            pltpu.VMEM((3, 2, 2, 3, 8, 256), f32),
            pltpu.VMEM((3, 2, 2, 3, 192, 256), i16),
            pltpu.VMEM((3, 2, 2, 3, 8, 256), f32),
            pltpu.VMEM((2, 3, 2, 192, 256), f32),
            pltpu.VMEM((3, 3, 192, 256), i16),
            pltpu.VMEM((3, 3, 8, 256), f32),
            pltpu.VMEM((3, 3, 192, 256), i16),
            pltpu.VMEM((3, 3, 8, 256), f32),
            pltpu.VMEM((2, 16, 768), f32),
            pltpu.VMEM((2, 4, 2, 16, 768), f32),
            pltpu.VMEM((3, 2, 2, 16, 768), f32),
            pltpu.VMEM((2, 2, 16, 768), f32),
            pltpu.VMEM((3, 16, 768), f32),
            pltpu.VMEM((2, 2, 4, 2, 16, 768), f32),
            pltpu.VMEM((PW, 768), bf16),
            pltpu.VMEM((PW, 768), bf16),
            pltpu.VMEM((PW, PW), f32),
            pltpu.VMEM((384, PW), i16),
            pltpu.VMEM((8, PW), f32),
            sems(1), sems(27), pltpu.SemaphoreType.DMA((9,)), sems(18), sems(18), sems(3), sems(3), sems(3),
            sems(6), sems(6), sems(9), sems(9), sems(9), sems(9),
            sems(32), sems(6), sems(3), sems(7), sems(1), sems(7), sems(7), sems(7),
        ],
        compiler_params=pltpu.CompilerParams(collective_id=0, has_side_effects=True, vmem_limit_bytes=LIMIT),
    )(structure, jnp.swapaxes(lower_panels, 2, 3), upper_panels, given_inverse, ancestor_entries)


def solution(mesh):
    return jax.shard_map(
        local,
        mesh=mesh,
        in_specs=(
            P("depth", None, None, ("rows", "cols")),
            P("depth", "rows", "cols"),
            P("depth", "rows", None),
            P("depth", None),
            P(("depth", "rows"), "cols"),
        ),
        out_specs=(P(("depth", "rows"), None), P(("depth", "rows"), "cols")),
        check_vma=False,
    )
```
